1024 devices in a mesh: dp: 32 (over y, z_hi, core), expert: 32 (over x, z_lo).
Axes of the slice: x: 8, y: 8, z: 8 (z_hi: 2, z_lo: 4; z = z_hi * 4 + z_lo), core: 2. Of those that a mesh axis runs over, the one named last changes fastest.
Arguments:
- tokens: bfloat16 [2, 8192, 2048], P(None, ('dp', 'expert')), may hold values from -6 to 6
- cotangent: bfloat16 [2, 8192, 2048], P(None, ('dp', 'expert')), may hold values from -6 to 6
- routes: int32 [2, 8192, 2], P(None, ('dp', 'expert')), may hold values from 0 to 15, all different within a row; in each aligned block of 8 rows (0 to 7, 8 to 15, ..., all dimensions but the last counted through in order) at most 2 rows name the same one
- gate_codes: int32 [2, 8192, 2], P(None, ('dp', 'expert')), may hold values from 1 to 255
- gate_weight: bfloat16 [32, 2048, 384], P('expert'), may hold values from -0.125 to 0.125
- up_weight: bfloat16 [32, 2048, 384], P('expert'), may hold values from -0.125 to 0.125
- down_weight: bfloat16 [32, 2048, 384], P('expert'), may hold values from -0.21875 to 0.21875
Outputs:
- mixed: bfloat16 [2, 8192, 2048], P(None, ('dp', 'expert'))
- grad_tokens: bfloat16 [2, 8192, 2048], P(None, ('dp', 'expert'))
- grad_gate: float32 [32, 2048, 384], P('expert', 'dp')
- grad_up: float32 [32, 2048, 384], P('expert', 'dp')
- grad_down: float32 [32, 2048, 384], P('expert', 'dp')
The draws below stay inside these ranges and needn't reach their ends.
Inputs may be any that keep to these rules, and one draw needn't show every extreme that they name: `routes`: in each micro-batch, the 8 tokens of one device name each expert at most 2 times in all; a token's 2 experts differ.
All inputs are finite; a program needn't handle non-finite values.
Results may differ from the reference program's by a relative error of at most 0.019.
Values may be sent and summed in bfloat16 or wider, within the bound.
A program may use at most 64 MiB of HBM per device.

```python
import math
from functools import partial
import jax
import jax.numpy as jnp
import numpy as np
from jax import lax

D = 2048
FF = 768
TOP = 2
MICRO = 2
TOK_MB = 8
EXPERTS = 16
FFH = 384
CAP = 2
TOTAL = 8192
EXPROWS = 4096
N_DP = 32
N_EXPERT = 32


def plant(drawn, stream_key, low, high):
    extent = drawn.shape
    spot = [jax.random.randint(jax.random.fold_in(stream_key, axis), (), 0, extent[axis]) for axis in range(len(extent))]
    drawn = drawn.at[tuple(spot)].set(low)
    longest = extent.index(max(extent))
    spot[longest] = (spot[longest] + 1) % extent[longest]
    return drawn.at[tuple(spot)].set(high)


def block_levels(own_key, extent, shards, low, largest):
    loudness = 1.0
    for axis_at, blocks in shards:
        draws = jax.random.uniform(jax.random.fold_in(jax.random.fold_in(own_key, 6), axis_at), (blocks,), jnp.float32, low / len(shards), largest / len(shards))
        loudness = loudness * jnp.repeat(jnp.exp(draws), extent[axis_at] // blocks).reshape((-1,) + (1,) * (len(extent) - 1 - axis_at))
    return loudness


def assign_block(stream_key, own, number, rows, number_of, top, reach, skew):
    ranking = jax.random.permutation(stream_key, number_of)
    packed, common = load_shares(number_of, rows * top, reach, skew, True), load_shares(number_of, rows * top, reach, skew, False)
    places = jnp.arange(number_of)

    def named(lengths, rotation):
        used = int((lengths > 0).sum())
        fixed = max(1, used // 4)
        moved = fixed + (places - fixed + rotation * (used - fixed)) % max(1, number_of - fixed)
        return jnp.zeros((number_of,), jnp.int32).at[ranking[jnp.where(places < fixed, places, moved)]].set(jnp.asarray(lengths, jnp.int32))

    lengths = jnp.where(number % 4 == 0, named(packed, number // 4), named(common, number - number // 4 - 1))
    mixed = jax.random.permutation(jax.random.fold_in(own, 3), number_of)
    donor, sink = mixed[0:number_of // 2 * 2:2], mixed[1:number_of // 2 * 2:2]
    room = jnp.minimum(lengths[donor] - 1, reach - lengths[sink]) // 2
    room = jnp.where((donor == ranking[0]) | (sink == ranking[0]) | (lengths[sink] == 0), 0, jnp.maximum(room, 0))
    moved = jax.random.randint(jax.random.fold_in(own, 4), (number_of // 2,), 0, 1 << 20) % (room + 1)
    lengths = lengths.at[donor].add(-moved).at[sink].add(moved)
    members = jnp.searchsorted(jnp.cumsum(lengths), jnp.arange(rows * top), side="right").astype(jnp.int32)
    grid = members.reshape(top, rows).T
    grid = grid[jax.random.permutation(jax.random.fold_in(own, 1), rows)]
    rotation = jax.random.randint(jax.random.fold_in(own, 2), (rows, 1), 0, top)
    return jnp.take_along_axis(grid, (jnp.arange(top)[None, :] + rotation) % top, axis=1)


def load_shares(count, total, most, slope, full):
    weights = [(1 << 20) // math.isqrt(grade ** slope) + 1 for grade in range(1, count + 1)]
    largest = most if full else min(most, max(-(-total // count), total * weights[0] // sum(weights)))
    least = 1 if total - largest >= count - 1 else 0
    given, spare = [largest] + [least] * (count - 1), total - largest - least * (count - 1)
    while spare > 0:
        candidates = [i for i in range(1, count) if given[i] < largest] or [i for i in range(1, count) if given[i] < most]
        pool, remaining = sum([weights[i] for i in candidates]), spare
        for i in candidates:
            more = min(most - given[i], max(1, remaining * weights[i] // pool), spare)
            given[i] = given[i] + more
            spare = spare - more
    return np.array(given)


def scatter_about(key, extent, width, most, pieces=(), kind=jnp.bfloat16):
    factor_of = block_levels(key, extent, pieces, -0.22, 0.18) if pieces else 1.0
    array = jax.random.normal(key, extent, jnp.float32) * width * factor_of
    return jnp.minimum(jnp.maximum(array, -most), most).astype(kind)


def setup_inputs(seed: int = 0) -> dict:
    arg_keys = jax.random.split(jax.random.key(seed), 8)
    tokens = scatter_about(arg_keys[0], (MICRO, TOTAL, D), 1.0, 6.0, ((1, 1024),))
    cotangent = scatter_about(arg_keys[1], (MICRO, TOTAL, D), 1.0, 6.0, ((1, 1024),))
    routes_keys = jax.random.split(jax.random.fold_in(arg_keys[2], 1), MICRO * TOTAL // TOK_MB)
    routes_turns = jax.random.permutation(jax.random.fold_in(arg_keys[2], 3), MICRO * TOTAL // TOK_MB)
    routes = jax.vmap(lambda own, number: assign_block(jax.random.fold_in(arg_keys[2], 2), own, number, TOK_MB, EXPERTS, TOP, CAP, 2))(routes_keys, routes_turns).reshape((MICRO, TOTAL, TOP))
    gate_codes = plant(jax.random.randint(arg_keys[3], (MICRO, TOTAL, TOP), 1, 256), jax.random.fold_in(arg_keys[3], 1), 1, 255).astype(jnp.int32)
    gate_weight = scatter_about(arg_keys[4], (2 * EXPERTS, D, FFH), D ** -0.5, 0.125, ((0, 32),))
    up_weight = scatter_about(arg_keys[5], (2 * EXPERTS, D, FFH), D ** -0.5, 0.125, ((0, 32),))
    down_weight = scatter_about(arg_keys[6], (2 * EXPERTS, D, FFH), FF ** -0.5, 0.21875, ((0, 32),))
    return dict(tokens=tokens, cotangent=cotangent, routes=routes, gate_codes=gate_codes, gate_weight=gate_weight, up_weight=up_weight, down_weight=down_weight)


def slot_tables(route_block, code_block, expert_count, capacity):
    tok_count, top_count = route_block.shape
    flat_routes = route_block.reshape(-1)
    onehot = (flat_routes[:, None] == jnp.arange(expert_count, dtype=jnp.int32)[None, :]).astype(jnp.int32)
    before = jnp.cumsum(onehot, axis=0) - onehot
    slot_rank = lax.optimization_barrier(jnp.sum(before * onehot, axis=1))
    slot_place = (slot_rank[:, None] == jnp.arange(capacity, dtype=jnp.int32)[None, :]).astype(jnp.float32)
    slot_mask = onehot.astype(jnp.float32)[:, :, None] * slot_place[:, None, :]
    slot_mask = slot_mask.reshape(tok_count, top_count, expert_count, capacity)
    code_float = code_block.astype(jnp.float32)
    share_table = code_float / lax.optimization_barrier(jnp.sum(code_float, axis=1, keepdims=True))
    select = lax.optimization_barrier(jnp.sum(slot_mask, axis=1))
    gate_share = lax.optimization_barrier(jnp.sum(share_table[:, :, None, None] * slot_mask, axis=1))
    return (select, gate_share)

def rounded(values):
    return lax.optimization_barrier(values.astype(jnp.bfloat16)).astype(jnp.float32)

def reference(tokens, cotangent, routes, gate_codes, gate_weight, up_weight, down_weight):
    half_hidden = FF // 2
    slot_total = N_EXPERT * CAP
    scale_factor = 1.0 / math.sqrt(EXPROWS)
    shape_five = (MICRO, N_DP, N_EXPERT, TOK_MB)
    token_all = tokens.reshape(shape_five + (D,)).transpose(1, 0, 2, 3, 4)
    cot_all = cotangent.reshape(shape_five + (D,)).transpose(1, 0, 2, 3, 4)
    route_all = routes.reshape(shape_five + (TOP,)).transpose(1, 0, 2, 3, 4)
    code_all = gate_codes.reshape(shape_five + (TOP,)).transpose(1, 0, 2, 3, 4)
    w_gate = gate_weight.reshape(EXPERTS, 2, D, half_hidden).astype(jnp.float32)
    w_up = up_weight.reshape(EXPERTS, 2, D, half_hidden).astype(jnp.float32)
    w_down = down_weight.reshape(EXPERTS, 2, D, half_hidden).astype(jnp.float32)
    tables = jax.vmap(partial(slot_tables, expert_count=EXPERTS, capacity=CAP))

    def dp_row_pass(grad_total, inputs):
        token_row, cot_row, route_row, code_row = inputs
        zeros_grad = jnp.zeros((EXPERTS, 2, D, half_hidden), jnp.float32)
        acc_gate, acc_up, acc_down = (zeros_grad, zeros_grad, zeros_grad)
        mixed_list = []
        back_list = []
        for micro_index in range(MICRO):
            select, gate_share = tables(route_row[micro_index], code_row[micro_index])
            rows_in = token_row[micro_index].astype(jnp.float32)
            cots_in = cot_row[micro_index].astype(jnp.float32)
            slot_rows = jnp.einsum('ktec,ktd->ekcd', select, rows_in, precision=lax.Precision.HIGHEST)
            slot_rows = slot_rows.reshape(EXPERTS, slot_total, D).astype(jnp.bfloat16).astype(jnp.float32)
            slot_share = lax.optimization_barrier(jnp.sum(gate_share, axis=1)).transpose(1, 0, 2)
            cot_slots = jnp.einsum('ktec,ktd->ekcd', select, cots_in, precision=lax.Precision.HIGHEST)
            slot_cots = rounded((slot_share[:, :, :, None] * cot_slots).reshape(EXPERTS, slot_total, D))
            pre_gate = jnp.einsum('erd,ehdf->ehrf', slot_rows, w_gate)
            pre_up = jnp.einsum('erd,ehdf->ehrf', slot_rows, w_up)
            sigma = jax.nn.sigmoid(pre_gate)
            activ = pre_gate * sigma
            hidden = rounded(activ * pre_up)
            out_parts = rounded(jnp.einsum('ehrf,ehdf->ehrd', hidden, w_down))
            grad_hidden = jnp.einsum('erd,ehdf->ehrf', slot_cots, w_down)
            grad_pre_gate = rounded(grad_hidden * pre_up * sigma * (1.0 + pre_gate * (1.0 - sigma)))
            grad_pre_up = rounded(grad_hidden * activ)
            grad_in = jnp.einsum('ehrf,ehdf->ehrd', grad_pre_gate, w_gate) + jnp.einsum('ehrf,ehdf->ehrd', grad_pre_up, w_up)
            grad_in = rounded(grad_in)
            acc_gate = acc_gate + jnp.einsum('erd,ehrf->ehdf', slot_rows, grad_pre_gate)
            acc_up = acc_up + jnp.einsum('erd,ehrf->ehdf', slot_rows, grad_pre_up)
            acc_down = acc_down + jnp.einsum('erd,ehrf->ehdf', slot_cots, hidden)
            out_sum = (out_parts[:, 0] + out_parts[:, 1]).reshape(EXPERTS, N_EXPERT, CAP, D)
            back_sum = (grad_in[:, 0] + grad_in[:, 1]).reshape(EXPERTS, N_EXPERT, CAP, D)
            mixed_part = jnp.einsum('ktec,ekcd->ktd', gate_share, out_sum, precision=lax.Precision.HIGHEST)
            back_part = jnp.einsum('ktec,ekcd->ktd', select, back_sum, precision=lax.Precision.HIGHEST)
            mixed_list.append(mixed_part.astype(jnp.bfloat16))
            back_list.append(back_part.astype(jnp.bfloat16))
        new_total = (grad_total[0] + rounded(acc_gate * scale_factor), grad_total[1] + rounded(acc_up * scale_factor), grad_total[2] + rounded(acc_down * scale_factor))
        return (new_total, (jnp.stack(mixed_list), jnp.stack(back_list)))
    zeros_total = jnp.zeros((EXPERTS, 2, D, half_hidden), jnp.float32)
    grad_total, outputs = lax.scan(dp_row_pass, (zeros_total, zeros_total, zeros_total), (token_all, cot_all, route_all, code_all))
    mixed = outputs[0].transpose(1, 0, 2, 3, 4).reshape(MICRO, TOTAL, D)
    grad_tokens = outputs[1].transpose(1, 0, 2, 3, 4).reshape(MICRO, TOTAL, D)
    grad_gate = grad_total[0].reshape(2 * EXPERTS, D, half_hidden)
    grad_up = grad_total[1].reshape(2 * EXPERTS, D, half_hidden)
    grad_down = grad_total[2].reshape(2 * EXPERTS, D, half_hidden)
    return (mixed, grad_tokens, grad_gate, grad_up, grad_down)
```

```python
import functools
import math

import jax
import jax.numpy as jnp
from jax import lax
from jax.experimental import pallas as pl
from jax.experimental.pallas import tpu as pltpu
from jax.sharding import PartitionSpec as P

MESH = pl.DeviceIdType.MESH
F32 = jnp.float32
BF16 = jnp.bfloat16


def dot(left, right):
    return jnp.dot(left, right, preferred_element_type=F32)


def dot_last(left, right):
    return lax.dot_general(left, right, (((1,), (1,)), ((), ())), preferred_element_type=F32)


def dot_first(left, right):
    return lax.dot_general(left, right, (((0,), (0,)), ((), ())), preferred_element_type=F32)


def iota(shape, axis):
    return lax.broadcasted_iota(jnp.int32, shape, axis)


def slot_ranks(cols, lanes):
    width = lanes.shape[1]
    tok_col = iota((16, width), 0)
    tok_lane = iota((16, width), 1) & 15
    same = (tok_col >> 3) == (tok_lane >> 3)
    before = same & (tok_col < tok_lane)
    upto = same & (tok_col <= tok_lane)
    col0, col1 = cols[:, 0:1], cols[:, 1:2]
    lane0, lane1 = lanes[0:1, :], lanes[1:2, :]

    def count(mask):
        return jnp.sum(jnp.where(mask, 1.0, 0.0), axis=0, keepdims=True)

    rank0 = count((col0 == lane0) & before) + count((col1 == lane0) & before)
    rank1 = count((col0 == lane1) & upto) + count((col1 == lane1) & before)
    return rank0, rank1


def slot_masks(rows, shift, cols, lanes):
    width = lanes.shape[1]
    rank0, rank1 = slot_ranks(cols, lanes)
    row = iota((rows, width), 0)
    lane = iota((rows, width), 1)
    expert = row >> shift
    slot = (row & 1).astype(F32)
    fits = (((row >> 2) & 3) == ((lane >> 4) & 3)) & (((row >> 1) & 1) == ((lane >> 3) & 1))
    mask0 = fits & (lanes[0:1, :] == expert) & (rank0 == slot)
    mask1 = fits & (lanes[1:2, :] == expert) & (rank1 == slot)
    return mask0, mask1


def kernel(
    scale_factor,
    n_dp,
    n_peer,
    cols_ref,
    lanes_ref,
    share_ref,
    tok_ref,
    cot_ref,
    wg_hbm,
    wu_hbm,
    wd_hbm,
    mixed_ref,
    back_ref,
    gg_ref,
    gu_ref,
    gd_ref,
    wg,
    wu,
    wd,
    outbox,
    inbox,
    xs,
    xt,
    xt_pair,
    gs,
    gs_pair,
    retbox,
    retin,
    comb,
    parts,
    ring,
    zbox,
    w_sem,
    fs_sem,
    fr_sem,
    rs_sem,
    rr_sem,
    cs_sem,
    cr_sem,
    ys_sem,
    yr_sem,
    zs_sem,
    zr_sem,
):
    k = lax.axis_index("expert")
    i = lax.axis_index("dp")
    n_y = n_dp // 4
    y, zh, core = i // 4, (i // 2) % 2, i % 2
    pair = y * 4 + zh * 2 + (1 - core)
    zpart = y * 4 + (1 - zh) * 2 + core
    up = ((y + 1) % n_y) * 4 + zh * 2 + core
    down = ((y + n_y - 1) % n_y) * 4 + zh * 2 + core

    w_copies = [
        pltpu.make_async_copy(src, dst, w_sem.at[n])
        for n, (src, dst) in enumerate(((wg_hbm, wg), (wu_hbm, wu), (wd_hbm, wd)))
    ]
    for copy in w_copies:
        copy.start()

    barrier = pltpu.get_barrier_semaphore()

    def greet(j, carry):
        pl.semaphore_signal(
            barrier, inc=1, device_id={"expert": (k + j) % n_peer}, device_id_type=MESH
        )
        return carry

    lax.fori_loop(1, n_peer, greet, 0)
    for other in (pair, zpart, up, down):
        pl.semaphore_signal(barrier, inc=1, device_id={"dp": other}, device_id_type=MESH)

    cols = cols_ref[...]
    lanes = lanes_ref[:, 0:64]
    share = share_ref[:, 0:64]
    mask0, mask1 = slot_masks(256, 4, cols, lanes)
    pick = jnp.where(mask0 | mask1, 1.0, 0.0).astype(BF16)
    slot_share = jnp.sum(
        jnp.where(mask0, share[0:1, :], 0.0) + jnp.where(mask1, share[1:2, :], 0.0),
        axis=1,
        keepdims=True,
    )
    is_cot = ((iota((256, 1), 0) >> 2) & 1) == 1
    slot_scale = jnp.where(is_cot, slot_share, 1.0)
    stack = jnp.concatenate(
        [tok_ref[:, 0:1024], cot_ref[:, 0:1024], tok_ref[:, 1024:2048], cot_ref[:, 1024:2048]],
        axis=0,
    )
    outbox[...] = (slot_scale * dot(pick, stack)).astype(BF16).reshape(16, 16, 1024)

    pl.semaphore_wait(barrier, n_peer - 1 + 4)

    def send_copy(j):
        peer = (k + j) % n_peer
        return pltpu.make_async_remote_copy(
            src_ref=outbox.at[peer // 2],
            dst_ref=inbox.at[k],
            send_sem=fs_sem.at[peer],
            recv_sem=fr_sem.at[k],
            device_id={"expert": peer},
            device_id_type=MESH,
        )

    def recv_copy(source):
        return pltpu.make_async_remote_copy(
            src_ref=outbox.at[0],
            dst_ref=inbox.at[source],
            send_sem=fs_sem.at[source],
            recv_sem=fr_sem.at[source],
            device_id={"expert": source},
            device_id_type=MESH,
        )

    def send_start(j, carry):
        send_copy(j).start()
        return carry

    lax.fori_loop(1, n_peer, send_start, 0)
    inbox[k] = outbox[k // 2]

    lanes = lanes_ref[...]
    lane = iota((2, 128), 1)
    weight = jnp.where(((lane >> 4) & 1) == 0, share_ref[...], 1.0)
    high = weight.astype(BF16).astype(F32)
    weight = jnp.where(lane < 64, high, weight - high)
    mask0, mask1 = slot_masks(512, 5, cols, lanes)
    comb[...] = (
        jnp.where(mask0, weight[0:1, :], 0.0) + jnp.where(mask1, weight[1:2, :], 0.0)
    ).astype(BF16)

    def recv_wait(j, carry):
        recv_copy((k + n_peer - j) % n_peer).wait_recv()
        return carry

    lax.fori_loop(1, n_peer, recv_wait, 0)

    row = iota((128, 128), 0)
    lane = iota((128, 128), 1)
    order = jnp.where(((row >> 2) & 7) * 16 + (row >> 5) * 4 + (row & 3) == lane, 1.0, 0.0)
    order = order.astype(BF16)
    for g in range(n_peer // 8):
        block = inbox[g * 8 : (g + 1) * 8].reshape(128, 1024)
        sorted_rows = dot(order, block).astype(BF16)
        for q in range(4):
            xs[q, g * 32 : (g + 1) * 32] = sorted_rows[q * 32 : (q + 1) * 32]

    for q in range(4):
        turned = jnp.transpose(xs[q])
        xt[q % 2, (q // 2) * 8 : (q // 2 + 1) * 8] = turned.reshape(8, 2, 64, 128)
    xt_copy = pltpu.make_async_remote_copy(
        src_ref=xt.at[:, :, 1 - core],
        dst_ref=xt_pair,
        send_sem=cs_sem.at[0],
        recv_sem=cr_sem.at[0],
        device_id={"dp": pair},
        device_id_type=MESH,
    )
    xt_copy.start()

    for copy in w_copies:
        copy.wait()

    pre_gate = dot(xs[0], wg[0:1024]) + dot(xs[2], wg[1024:2048])
    pre_up = dot(xs[0], wu[0:1024]) + dot(xs[2], wu[1024:2048])
    grad_hidden = dot(xs[1], wd[0:1024]) + dot(xs[3], wd[1024:2048])
    sigma = jax.nn.sigmoid(pre_gate)
    activ = pre_gate * sigma
    hidden = (activ * pre_up).astype(BF16)
    grad_gate = (grad_hidden * pre_up * sigma * (1.0 + pre_gate * (1.0 - sigma))).astype(BF16)
    grad_up = (grad_hidden * activ).astype(BF16)
    gs[0] = grad_gate
    gs[1] = grad_up
    gs[2] = hidden
    gs_copy = pltpu.make_async_remote_copy(
        src_ref=gs,
        dst_ref=gs_pair,
        send_sem=cs_sem.at[1],
        recv_sem=cr_sem.at[1],
        device_id={"dp": pair},
        device_id_type=MESH,
    )
    gs_copy.start()

    for d in range(2):
        half = slice(d * 1024, (d + 1) * 1024)
        xs[2 * d] = dot_last(hidden, wd[half]).astype(BF16)
        xs[2 * d + 1] = (dot_last(grad_gate, wg[half]) + dot_last(grad_up, wu[half])).astype(BF16)
    back_order = jnp.where(((lane >> 2) & 7) * 16 + (lane >> 5) * 4 + (lane & 3) == row, 1.0, 0.0)
    back_order = back_order.astype(BF16)
    for g in range(n_peer // 8):
        block = jnp.concatenate([xs[q, g * 32 : (g + 1) * 32] for q in range(4)], axis=0)
        retbox[g * 8 : (g + 1) * 8] = dot(back_order, block).astype(BF16).reshape(8, 16, 1024)

    def ret_copy(j):
        peer = (k + j) % n_peer
        return pltpu.make_async_remote_copy(
            src_ref=retbox.at[peer],
            dst_ref=retin.at[k],
            send_sem=rs_sem.at[peer],
            recv_sem=rr_sem.at[k],
            device_id={"expert": peer},
            device_id_type=MESH,
        )

    def ret_recv(source):
        return pltpu.make_async_remote_copy(
            src_ref=retbox.at[source],
            dst_ref=retin.at[source],
            send_sem=rs_sem.at[source],
            recv_sem=rr_sem.at[source],
            device_id={"expert": source},
            device_id_type=MESH,
        )

    def ret_start(j, carry):
        ret_copy(j).start()
        return carry

    lax.fori_loop(1, n_peer, ret_start, 0)
    retin[k] = retbox[k]

    xt_copy.wait_recv()
    gs_copy.wait_recv()
    for n in range(3):
        a = 0 if n < 2 else 1
        left = jnp.concatenate(
            [xt[a, :, core].reshape(1024, 128), xt_pair[a].reshape(1024, 128)], axis=1
        )
        right = jnp.concatenate([gs[n], gs_pair[n]], axis=0)
        part = (dot(left, right) * scale_factor).astype(BF16)
        parts[:, n * 64 : (n + 1) * 64] = part.reshape(16, 64, 384)

    streams = [(part_at, d) for part_at in range(2) for d in range(2)]

    def own_piece(part_at, d, step):
        side = 1 - zh if part_at == 0 else zh
        at = (y + 2 * n_y - 1 - step) % n_y if d == 0 else (y + 1 + step) % n_y
        return parts.at[at * 2 + side, pl.ds(d * 96, 96)]

    def ring_copy(n, source, step):
        return pltpu.make_async_remote_copy(
            src_ref=source,
            dst_ref=ring.at[n, step],
            send_sem=ys_sem.at[n, step],
            recv_sem=yr_sem.at[n, step],
            device_id={"dp": up if streams[n][1] == 0 else down},
            device_id_type=MESH,
        )

    for n, (part_at, d) in enumerate(streams):
        ring_copy(n, own_piece(part_at, d, 0), 0).start()

    def ring_add(n, step):
        part_at, d = streams[n]
        ring_copy(n, ring.at[n, step], step).wait_recv()
        ring[n, step] = (
            ring[n, step].astype(F32) + own_piece(part_at, d, step + 1)[...].astype(F32)
        ).astype(BF16)

    def ring_step(step, carry):
        for n in range(4):
            ring_add(n, step)
            ring_copy(n, ring.at[n, step], step + 1).start()
        return carry

    last = n_y - 2
    lax.fori_loop(0, last, ring_step, 0)

    z_copies = [
        pltpu.make_async_remote_copy(
            src_ref=ring.at[d, last],
            dst_ref=zbox.at[d],
            send_sem=zs_sem.at[d],
            recv_sem=zr_sem.at[d],
            device_id={"dp": zpart},
            device_id_type=MESH,
        )
        for d in range(2)
    ]
    for d in range(2):
        ring_add(d, last)
        z_copies[d].start()

    def ret_wait(j, carry):
        ret_recv((k + n_peer - j) % n_peer).wait_recv()
        return carry

    lax.fori_loop(1, n_peer, ret_wait, 0)
    both = dot_first(comb[...], retin[...].reshape(512, 1024))
    total = (both[0:64] + both[64:128]).astype(BF16)
    mixed_ref[:, 0:1024] = total[0:16]
    back_ref[:, 0:1024] = total[16:32]
    mixed_ref[:, 1024:2048] = total[32:48]
    back_ref[:, 1024:2048] = total[48:64]

    sums = []
    for d in range(2):
        n = 2 + d
        ring_copy(n, ring.at[n, last], last).wait_recv()
        own = ring[n, last].astype(F32) + own_piece(1, d, last + 1)[...].astype(F32)
        z_copies[d].wait_recv()
        sums.append(own + zbox[d].astype(F32))
    gg_ref[...] = sums[0][0:64]
    gu_ref[0:32] = sums[0][64:96]
    gu_ref[32:64] = sums[1][0:32]
    gd_ref[...] = sums[1][32:96]

    def send_wait(j, carry):
        send_copy(j).wait_send()
        ret_copy(j).wait_send()
        return carry

    lax.fori_loop(1, n_peer, send_wait, 0)
    xt_copy.wait_send()
    gs_copy.wait_send()

    def ring_wait(step, carry):
        for n in range(4):
            ring_copy(n, ring.at[n, step], step).wait_send()
        return carry

    lax.fori_loop(0, last + 1, ring_wait, 0)
    for copy in z_copies:
        copy.wait_send()


def shards(tokens, cotangent, routes, gate_codes, gate_weight, up_weight, down_weight):
    micro, toks, width = tokens.shape
    n_peer = lax.axis_size("expert")
    n_dp = lax.axis_size("dp")
    hidden = gate_weight.shape[2]
    rows = micro * toks
    scale_factor = 1.0 / math.sqrt(n_dp * micro * n_peer * 2)
    cols = routes.reshape(rows, 2)
    codes = gate_codes.reshape(rows, 2).astype(F32)
    share = codes / jnp.sum(codes, axis=1, keepdims=True)
    lanes = jnp.tile(cols.T, (1, 8))
    share = jnp.tile(share.T, (1, 8))
    n_y = n_dp // 4
    vmem = pl.BlockSpec(memory_space=pltpu.VMEM)
    anyspace = pl.BlockSpec(memory_space=pl.ANY)
    dma = pltpu.SemaphoreType.DMA
    grad = jax.ShapeDtypeStruct((width // n_dp, hidden), F32)
    mixed, back, gg, gu, gd = pl.pallas_call(
        functools.partial(kernel, scale_factor, n_dp, n_peer),
        out_shape=(
            jax.ShapeDtypeStruct((rows, width), BF16),
            jax.ShapeDtypeStruct((rows, width), BF16),
            grad,
            grad,
            grad,
        ),
        in_specs=[vmem] * 5 + [anyspace] * 3,
        out_specs=(vmem,) * 5,
        scratch_shapes=[
            pltpu.VMEM((width, hidden), BF16),
            pltpu.VMEM((width, hidden), BF16),
            pltpu.VMEM((width, hidden), BF16),
            pltpu.VMEM((n_peer // 2, 16, 1024), BF16),
            pltpu.VMEM((n_peer, 16, 1024), BF16),
            pltpu.VMEM((4, 128, 1024), BF16),
            pltpu.VMEM((2, 16, 2, 64, 128), BF16),
            pltpu.VMEM((2, 16, 64, 128), BF16),
            pltpu.VMEM((3, 128, hidden), BF16),
            pltpu.VMEM((3, 128, hidden), BF16),
            pltpu.VMEM((n_peer, 16, 1024), BF16),
            pltpu.VMEM((n_peer, 16, 1024), BF16),
            pltpu.VMEM((512, 128), BF16),
            pltpu.VMEM((16, 192, hidden), BF16),
            pltpu.VMEM((4, n_y - 1, 96, hidden), BF16),
            pltpu.VMEM((2, 96, hidden), BF16),
            dma((3,)),
            dma((n_peer,)),
            dma((n_peer,)),
            dma((n_peer,)),
            dma((n_peer,)),
            dma((2,)),
            dma((2,)),
            dma((4, n_y - 1)),
            dma((4, n_y - 1)),
            dma((2,)),
            dma((2,)),
        ],
        compiler_params=pltpu.CompilerParams(
            collective_id=0, has_side_effects=True, vmem_limit_bytes=48 * 1024 * 1024
        ),
        name="moe_layer",
    )(
        cols,
        lanes,
        share,
        tokens.reshape(rows, width),
        cotangent.reshape(rows, width),
        gate_weight[0],
        up_weight[0],
        down_weight[0],
    )
    shape = (micro, toks, width)
    return mixed.reshape(shape), back.reshape(shape), gg[None], gu[None], gd[None]


def solution(mesh):
    tok_spec = P(None, ("dp", "expert"), None)
    w_spec = P("expert", None, None)
    g_spec = P("expert", "dp", None)
    return jax.shard_map(
        shards,
        mesh=mesh,
        in_specs=(tok_spec,) * 4 + (w_spec,) * 3,
        out_specs=(tok_spec,) * 2 + (g_spec,) * 3,
        check_vma=False,
    )
```

```python
import functools
import math

import jax
import jax.numpy as jnp
from jax import lax
from jax.experimental import pallas as pl
from jax.experimental.pallas import tpu as pltpu
from jax.sharding import PartitionSpec as P

MESH = pl.DeviceIdType.MESH
F32 = jnp.float32
BF16 = jnp.bfloat16

ORDER = (0, 1, 7, 2, 6, 3, 5, 4)


def dot(left, right):
    return jnp.dot(left, right, preferred_element_type=F32)


def dot_last(left, right):
    return lax.dot_general(left, right, (((1,), (1,)), ((), ())), preferred_element_type=F32)


def dot_first(left, right):
    return lax.dot_general(left, right, (((0,), (0,)), ((), ())), preferred_element_type=F32)


def iota(shape, axis):
    return lax.broadcasted_iota(jnp.int32, shape, axis)


def route_vectors(route_ref, code_ref):
    row = iota((16, 8), 0)
    lane = iota((16, 8), 1)
    here = [(lane == (row & 7)) & ((row >> 3) == m) for m in range(2)]

    def column(ref, r):
        parts = [jnp.where(here[m], ref[m, r : r + 1, :].astype(F32), 0.0) for m in range(2)]
        return jnp.sum(parts[0] + parts[1], axis=1, keepdims=True)

    spread = iota((16, 128), 0) == (iota((16, 128), 1) & 15)

    def along(col):
        return jnp.sum(jnp.where(spread, col, 0.0), axis=0, keepdims=True)

    cols = [column(route_ref, r) for r in range(2)]
    codes = [column(code_ref, r) for r in range(2)]
    whole = codes[0] + codes[1]
    lanes = jnp.concatenate([along(col) for col in cols], axis=0)
    share = jnp.concatenate([along(code / whole) for code in codes], axis=0)
    return jnp.concatenate(cols, axis=1), lanes, share


def slot_ranks(cols, lanes):
    width = lanes.shape[1]
    tok_col = iota((16, width), 0)
    tok_lane = iota((16, width), 1) & 15
    same = (tok_col >> 3) == (tok_lane >> 3)
    before = same & (tok_col < tok_lane)
    upto = same & (tok_col <= tok_lane)
    col0, col1 = cols[:, 0:1], cols[:, 1:2]
    lane0, lane1 = lanes[0:1, :], lanes[1:2, :]

    def count(mask):
        return jnp.sum(jnp.where(mask, 1.0, 0.0), axis=0, keepdims=True)

    rank0 = count((col0 == lane0) & before) + count((col1 == lane0) & before)
    rank1 = count((col0 == lane1) & upto) + count((col1 == lane1) & before)
    return rank0, rank1


def slot_masks(rows, shift, cols, lanes):
    width = lanes.shape[1]
    rank0, rank1 = slot_ranks(cols, lanes)
    row = iota((rows, width), 0)
    lane = iota((rows, width), 1)
    expert = (row >> shift).astype(F32)
    slot = (row & 1).astype(F32)
    fits = (((row >> 2) & 3) == ((lane >> 4) & 3)) & (((row >> 1) & 1) == ((lane >> 3) & 1))
    mask0 = fits & (lanes[0:1, :] == expert) & (rank0 == slot)
    mask1 = fits & (lanes[1:2, :] == expert) & (rank1 == slot)
    return mask0, mask1


def kernel(
    scale_factor,
    n_dp,
    n_peer,
    route_hbm,
    code_hbm,
    tok_hbm,
    cot_hbm,
    wg_hbm,
    wu_hbm,
    wd_hbm,
    mixed_ref,
    back_ref,
    gg_ref,
    gu_ref,
    gd_ref,
    route_ref,
    code_ref,
    tok_ref,
    cot_ref,
    wg,
    wu,
    wd,
    outbox,
    relay,
    inbox,
    xs,
    xt,
    xt_pair,
    gs,
    gs_pair,
    retbox,
    retin,
    comb,
    parts,
    ring,
    zbox,
    w_sem,
    xs_sem,
    xr_sem,
    ps_sem,
    os_sem,
    hs_sem,
    pr_sem,
    rs_sem,
    rr_sem,
    cs_sem,
    cr_sem,
    ys_sem,
    yr_sem,
    zs_sem,
    zr_sem,
):
    k = lax.axis_index("expert")
    i = lax.axis_index("dp")
    n_y = n_dp // 4
    n_x = n_peer // 4
    x, z = k // 4, k % 4
    y, zh, core = i // 4, (i // 2) % 2, i % 2
    pair = y * 4 + zh * 2 + (1 - core)
    zpart = y * 4 + (1 - zh) * 2 + core
    up = ((y + 1) % n_y) * 4 + zh * 2 + core
    down = ((y + n_y - 1) % n_y) * 4 + zh * 2 + core

    loads = (
        (route_hbm, route_ref),
        (code_hbm, code_ref),
        (tok_hbm, tok_ref),
        (cot_hbm, cot_ref),
        (wg_hbm.at[0], wg),
        (wu_hbm.at[0], wu),
        (wd_hbm.at[0], wd),
    )
    loads = [pltpu.make_async_copy(src, dst, w_sem.at[n]) for n, (src, dst) in enumerate(loads)]
    t_copies, w_copies = loads[:4], loads[4:]
    for copy in loads:
        copy.start()

    barrier = pltpu.get_barrier_semaphore()

    def greet(j, carry):
        pl.semaphore_signal(
            barrier, inc=1, device_id={"expert": (k + j) % n_peer}, device_id_type=MESH
        )
        return carry

    lax.fori_loop(1, n_peer, greet, 0)
    for other in (pair, zpart, up, down):
        pl.semaphore_signal(barrier, inc=1, device_id={"dp": other}, device_id_type=MESH)

    for copy in t_copies:
        copy.wait()

    cols, all_lanes, all_share = route_vectors(route_ref, code_ref)
    lanes = all_lanes[:, 0:64]
    share = all_share[:, 0:64]
    mask0, mask1 = slot_masks(256, 4, cols, lanes)
    pick = jnp.where(mask0 | mask1, 1.0, 0.0).astype(BF16)
    slot_share = jnp.sum(
        jnp.where(mask0, share[0:1, :], 0.0) + jnp.where(mask1, share[1:2, :], 0.0),
        axis=1,
        keepdims=True,
    )
    is_cot = ((iota((256, 1), 0) >> 2) & 1) == 1
    slot_scale = jnp.where(is_cot, slot_share, 1.0)
    stack = jnp.concatenate(
        [
            ref[m, :, d * 1024 : (d + 1) * 1024]
            for d in range(2)
            for ref in (tok_ref, cot_ref)
            for m in range(2)
        ],
        axis=0,
    )
    outbox[...] = (slot_scale * dot(pick, stack)).astype(BF16).reshape(16, 16, 1024)

    pl.semaphore_wait(barrier, n_peer - 1 + 4)

    def over_x(at):
        return pltpu.make_async_remote_copy(
            src_ref=outbox.at[pl.ds((x + ORDER[at]) % n_x * 2, 2)],
            dst_ref=relay.at[at],
            send_sem=xs_sem.at[at],
            recv_sem=xr_sem.at[at],
            device_id={"expert": (x + ORDER[at]) % n_x * 4 + z},
            device_id_type=MESH,
        )

    def to_pair(at):
        return pltpu.make_async_remote_copy(
            src_ref=relay.at[at, z // 2],
            dst_ref=inbox.at[at, z],
            send_sem=ps_sem.at[at],
            recv_sem=pr_sem.at[at, z],
            device_id={"expert": x * 4 + z + 1 - z % 2 * 2},
            device_id_type=MESH,
        )

    def to_other(at):
        return pltpu.make_async_remote_copy(
            src_ref=relay.at[at, 1 - z // 2],
            dst_ref=inbox.at[at, z],
            send_sem=os_sem.at[at],
            recv_sem=pr_sem.at[at, z],
            device_id={"expert": x * 4 + (1 - z // 2) * 2 + at % 2},
            device_id_type=MESH,
        )

    def hand_on(turn, b):
        at = turn * 2 + z % 2
        source = (1 - z // 2) * 2 + b
        return pltpu.make_async_remote_copy(
            src_ref=inbox.at[at, source],
            dst_ref=inbox.at[at, source],
            send_sem=hs_sem.at[turn, b],
            recv_sem=pr_sem.at[at, source],
            device_id={"expert": x * 4 + z + 1 - z % 2 * 2},
            device_id_type=MESH,
        )

    def arrival(at, source):
        return pltpu.make_async_remote_copy(
            src_ref=inbox.at[at, source],
            dst_ref=inbox.at[at, source],
            send_sem=ps_sem.at[0],
            recv_sem=pr_sem.at[at, source],
            device_id={"expert": x * 4 + z + 1 - z % 2 * 2},
            device_id_type=MESH,
        )

    for at in range(1, n_x):
        over_x(at).start()
    relay[0] = outbox[pl.ds(x * 2, 2)]

    lane = iota((2, 128), 1)
    weight = jnp.where(((lane >> 4) & 1) == 0, all_share, 1.0)
    high = weight.astype(BF16).astype(F32)
    weight = jnp.where(lane < 64, high, weight - high)
    mask0, mask1 = slot_masks(512, 5, cols, all_lanes)
    comb[...] = (
        jnp.where(mask0, weight[0:1, :], 0.0) + jnp.where(mask1, weight[1:2, :], 0.0)
    ).astype(BF16)

    row = iota((128, 128), 0)
    lane = iota((128, 128), 1)
    order = jnp.where(((row >> 2) & 7) * 16 + (row >> 5) * 4 + (row & 3) == lane, 1.0, 0.0)
    order = order.astype(BF16)

    def forward(at):
        if at:
            over_x(at).wait_recv()
        to_pair(at).start()
        to_other(at).start()
        inbox[at, z] = relay[at, z // 2]

    def relay_turn(turn):
        for b in range(2):
            arrival(turn * 2 + z % 2, (1 - z // 2) * 2 + b).wait_recv()
            hand_on(turn, b).start()

    def sort_rows(g):
        for at in (2 * g, 2 * g + 1):
            arrival(at, z + 1 - z % 2 * 2).wait_recv()
        for b in range(2):
            arrival(2 * g + 1 - z % 2, (1 - z // 2) * 2 + b).wait_recv()
        block = inbox[2 * g : 2 * g + 2].reshape(128, 1024)
        sorted_rows = dot(order, block).astype(BF16)
        for q in range(4):
            xs[q, g * 32 : (g + 1) * 32] = sorted_rows[q * 32 : (q + 1) * 32]

    forward(0)
    forward(1)
    forward(2)
    relay_turn(0)
    forward(3)
    forward(4)
    relay_turn(1)
    forward(5)
    forward(6)
    relay_turn(2)
    sort_rows(0)
    forward(7)
    sort_rows(1)
    relay_turn(3)
    sort_rows(2)
    sort_rows(3)

    for copy in w_copies:
        copy.wait()

    pre_gate = dot(xs[0], wg[0:1024]) + dot(xs[2], wg[1024:2048])
    pre_up = dot(xs[0], wu[0:1024]) + dot(xs[2], wu[1024:2048])
    grad_hidden = dot(xs[1], wd[0:1024]) + dot(xs[3], wd[1024:2048])
    sigma = jax.nn.sigmoid(pre_gate)
    activ = pre_gate * sigma
    hidden = (activ * pre_up).astype(BF16)
    grad_gate = (grad_hidden * pre_up * sigma * (1.0 + pre_gate * (1.0 - sigma))).astype(BF16)
    grad_up = (grad_hidden * activ).astype(BF16)
    gs[0] = grad_gate
    gs[1] = grad_up
    gs[2] = hidden
    gs_copy = pltpu.make_async_remote_copy(
        src_ref=gs,
        dst_ref=gs_pair,
        send_sem=cs_sem.at[1],
        recv_sem=cr_sem.at[1],
        device_id={"dp": pair},
        device_id_type=MESH,
    )
    gs_copy.start()

    for q in range(4):
        turned = jnp.transpose(xs[q])
        xt[q % 2, (q // 2) * 8 : (q // 2 + 1) * 8] = turned.reshape(8, 2, 64, 128)
    xt_copy = pltpu.make_async_remote_copy(
        src_ref=xt.at[:, :, 1 - core],
        dst_ref=xt_pair,
        send_sem=cs_sem.at[0],
        recv_sem=cr_sem.at[0],
        device_id={"dp": pair},
        device_id_type=MESH,
    )
    xt_copy.start()

    xt_copy.wait_recv()
    gs_copy.wait_recv()
    for n in range(3):
        a = 0 if n < 2 else 1
        left = jnp.concatenate(
            [xt[a, :, core].reshape(1024, 128), xt_pair[a].reshape(1024, 128)], axis=1
        )
        right = jnp.concatenate([gs[n], gs_pair[n]], axis=0)
        part = (dot(left, right) * scale_factor).astype(BF16)
        parts[:, n * 64 : (n + 1) * 64] = part.reshape(16, 64, 384)

    streams = [(part_at, d) for part_at in range(2) for d in range(2)]

    def own_piece(part_at, d, step):
        side = 1 - zh if part_at == 0 else zh
        at = (y + 2 * n_y - 1 - step) % n_y if d == 0 else (y + 1 + step) % n_y
        return parts.at[at * 2 + side, pl.ds(d * 96, 96)]

    def ring_copy(n, source, step):
        return pltpu.make_async_remote_copy(
            src_ref=source,
            dst_ref=ring.at[n, step],
            send_sem=ys_sem.at[n, step],
            recv_sem=yr_sem.at[n, step],
            device_id={"dp": up if streams[n][1] == 0 else down},
            device_id_type=MESH,
        )

    for n, (part_at, d) in enumerate(streams):
        ring_copy(n, own_piece(part_at, d, 0), 0).start()

    for d in range(2):
        half = slice(d * 1024, (d + 1) * 1024)
        xs[2 * d] = dot_last(hidden, wd[half]).astype(BF16)
        xs[2 * d + 1] = (dot_last(grad_gate, wg[half]) + dot_last(grad_up, wu[half])).astype(BF16)
    back_order = jnp.where(((lane >> 2) & 7) * 16 + (lane >> 5) * 4 + (lane & 3) == row, 1.0, 0.0)
    back_order = back_order.astype(BF16)
    for g in range(n_peer // 8):
        block = jnp.concatenate([xs[q, g * 32 : (g + 1) * 32] for q in range(4)], axis=0)
        retbox[2 * g : 2 * g + 2] = dot(back_order, block).astype(BF16).reshape(2, 4, 16, 1024)

    def ret_copy(at, source):
        return pltpu.make_async_remote_copy(
            src_ref=retbox.at[at, source],
            dst_ref=retin.at[k],
            send_sem=rs_sem.at[at, source],
            recv_sem=rr_sem.at[k],
            device_id={"expert": (x + n_x - ORDER[at]) % n_x * 4 + source},
            device_id_type=MESH,
        )

    def ret_recv(source):
        return pltpu.make_async_remote_copy(
            src_ref=retin.at[source],
            dst_ref=retin.at[source],
            send_sem=rs_sem.at[0, 0],
            recv_sem=rr_sem.at[source],
            device_id={"expert": source},
            device_id_type=MESH,
        )

    def ret_sends():
        return [(0, (z + n) % 4) for n in range(1, 4)] + [
            (at, (z + n) % 4) for at in range(1, n_x) for n in range(4)
        ]

    for at, source in ret_sends():
        ret_copy(at, source).start()
    retin[k] = retbox[0, z]

    def ring_add(n, step):
        part_at, d = streams[n]
        ring_copy(n, ring.at[n, step], step).wait_recv()
        ring[n, step] = (
            ring[n, step].astype(F32) + own_piece(part_at, d, step + 1)[...].astype(F32)
        ).astype(BF16)

    def ring_step(step, carry):
        for n in range(4):
            ring_add(n, step)
            ring_copy(n, ring.at[n, step], step + 1).start()
        return carry

    last = n_y - 2
    lax.fori_loop(0, last, ring_step, 0)

    z_copies = [
        pltpu.make_async_remote_copy(
            src_ref=ring.at[d, last],
            dst_ref=zbox.at[d],
            send_sem=zs_sem.at[d],
            recv_sem=zr_sem.at[d],
            device_id={"dp": zpart},
            device_id_type=MESH,
        )
        for d in range(2)
    ]
    for d in range(2):
        ring_add(d, last)
        z_copies[d].start()

    def ret_wait(j, carry):
        ret_recv((k + n_peer - j) % n_peer).wait_recv()
        return carry

    lax.fori_loop(1, n_peer, ret_wait, 0)
    both = dot_first(comb[...], retin[...].reshape(512, 1024))
    total = (both[0:64] + both[64:128]).astype(BF16)
    for m in range(2):
        for d in range(2):
            half = slice(d * 1024, (d + 1) * 1024)
            at = d * 32 + m * 8
            mixed_ref[m, :, half] = total[at : at + 8]
            back_ref[m, :, half] = total[at + 16 : at + 24]

    sums = []
    for d in range(2):
        n = 2 + d
        ring_copy(n, ring.at[n, last], last).wait_recv()
        own = ring[n, last].astype(F32) + own_piece(1, d, last + 1)[...].astype(F32)
        z_copies[d].wait_recv()
        sums.append(own + zbox[d].astype(F32))
    gg_ref[0] = sums[0][0:64]
    gu_ref[0, 0:32] = sums[0][64:96]
    gu_ref[0, 32:64] = sums[1][0:32]
    gd_ref[0] = sums[1][32:96]

    for at in range(n_x):
        if at:
            over_x(at).wait_send()
        to_pair(at).wait_send()
        to_other(at).wait_send()
    for turn in range(n_x // 2):
        for b in range(2):
            hand_on(turn, b).wait_send()
    for at, source in ret_sends():
        ret_copy(at, source).wait_send()
    xt_copy.wait_send()
    gs_copy.wait_send()

    def ring_wait(step, carry):
        for n in range(4):
            ring_copy(n, ring.at[n, step], step).wait_send()
        return carry

    lax.fori_loop(0, last + 1, ring_wait, 0)
    for copy in z_copies:
        copy.wait_send()


def write_kernel(count, *refs):
    ins, outs, held = refs[:count], refs[count : 2 * count], refs[2 * count : 3 * count]
    in_sem, out_sem = refs[3 * count :]
    reads = [pltpu.make_async_copy(ins[n], held[n], in_sem.at[n]) for n in range(count)]
    writes = [pltpu.make_async_copy(held[n], outs[n], out_sem.at[n]) for n in range(count)]
    for copy in reads:
        copy.start()
    for n in range(count):
        reads[n].wait()
        writes[n].start()
    for copy in writes:
        copy.wait()


def shards(tokens, cotangent, routes, gate_codes, gate_weight, up_weight, down_weight):
    micro, toks, width = tokens.shape
    n_peer = lax.axis_size("expert")
    n_dp = lax.axis_size("dp")
    hidden = gate_weight.shape[2]
    scale_factor = 1.0 / math.sqrt(n_dp * micro * n_peer * 2)
    n_y = n_dp // 4
    n_x = n_peer // 4
    vmem = pl.BlockSpec(memory_space=pltpu.VMEM)
    hbm = pl.BlockSpec(memory_space=pltpu.HBM)
    anyspace = pl.BlockSpec(memory_space=pl.ANY)
    dma = pltpu.SemaphoreType.DMA
    tok = jax.ShapeDtypeStruct((micro, toks, width), BF16)
    grad = jax.ShapeDtypeStruct((1, width // n_dp, hidden), F32)
    shapes = (tok, tok, grad, grad, grad)
    results = pl.pallas_call(
        functools.partial(kernel, scale_factor, n_dp, n_peer),
        out_shape=shapes,
        in_specs=[hbm] * 7,
        out_specs=(vmem,) * 5,
        scratch_shapes=[
            pltpu.VMEM((micro, 2, toks), jnp.int32),
            pltpu.VMEM((micro, 2, toks), jnp.int32),
            pltpu.VMEM((micro, toks, width), BF16),
            pltpu.VMEM((micro, toks, width), BF16),
            pltpu.VMEM((width, hidden), BF16),
            pltpu.VMEM((width, hidden), BF16),
            pltpu.VMEM((width, hidden), BF16),
            pltpu.VMEM((n_peer // 2, 16, 1024), BF16),
            pltpu.VMEM((n_x, 2, 16, 1024), BF16),
            pltpu.VMEM((n_x, 4, 16, 1024), BF16),
            pltpu.VMEM((4, 128, 1024), BF16),
            pltpu.VMEM((2, 16, 2, 64, 128), BF16),
            pltpu.VMEM((2, 16, 64, 128), BF16),
            pltpu.VMEM((3, 128, hidden), BF16),
            pltpu.VMEM((3, 128, hidden), BF16),
            pltpu.VMEM((n_x, 4, 16, 1024), BF16),
            pltpu.VMEM((n_peer, 16, 1024), BF16),
            pltpu.VMEM((512, 128), BF16),
            pltpu.VMEM((16, 192, hidden), BF16),
            pltpu.VMEM((4, n_y - 1, 96, hidden), BF16),
            pltpu.VMEM((2, 96, hidden), BF16),
            dma((7,)),
            dma((n_x,)),
            dma((n_x,)),
            dma((n_x,)),
            dma((n_x,)),
            dma((n_x // 2, 2)),
            dma((n_x, 4)),
            dma((n_x, 4)),
            dma((n_peer,)),
            dma((2,)),
            dma((2,)),
            dma((4, n_y - 1)),
            dma((4, n_y - 1)),
            dma((2,)),
            dma((2,)),
        ],
        compiler_params=pltpu.CompilerParams(
            collective_id=0, has_side_effects=True, vmem_limit_bytes=56 * 1024 * 1024
        ),
        name="moe_layer",
    )(
        routes.transpose(0, 2, 1),
        gate_codes.transpose(0, 2, 1),
        tokens,
        cotangent,
        gate_weight,
        up_weight,
        down_weight,
    )
    return pl.pallas_call(
        functools.partial(write_kernel, len(shapes)),
        out_shape=shapes,
        in_specs=[anyspace] * len(shapes),
        out_specs=(hbm,) * len(shapes),
        scratch_shapes=[pltpu.VMEM(one.shape, one.dtype) for one in shapes]
        + [dma((len(shapes),)), dma((len(shapes),))],
        name="write_out",
    )(*results)


def solution(mesh):
    tok_spec = P(None, ("dp", "expert"), None)
    w_spec = P("expert", None, None)
    g_spec = P("expert", "dp", None)
    return jax.shard_map(
        shards,
        mesh=mesh,
        in_specs=(tok_spec,) * 4 + (w_spec,) * 3,
        out_specs=(tok_spec,) * 2 + (g_spec,) * 3,
        check_vma=False,
    )
```

```python
import functools
import math

import jax
import jax.numpy as jnp
from jax import lax
from jax.experimental import pallas as pl
from jax.experimental.pallas import tpu as pltpu
from jax.sharding import PartitionSpec as P

MESH = pl.DeviceIdType.MESH
F32 = jnp.float32
BF16 = jnp.bfloat16

ORDER = (0, 1, 7, 2, 6, 3, 5, 4)


def dot(left, right):
    return jnp.dot(left, right, preferred_element_type=F32)


def dot_last(left, right):
    return lax.dot_general(left, right, (((1,), (1,)), ((), ())), preferred_element_type=F32)


def dot_first(left, right):
    return lax.dot_general(left, right, (((0,), (0,)), ((), ())), preferred_element_type=F32)


def iota(shape, axis):
    return lax.broadcasted_iota(jnp.int32, shape, axis)


def route_vectors(route_ref, code_ref):
    row = iota((16, 8), 0)
    lane = iota((16, 8), 1)
    here = [(lane == (row & 7)) & ((row >> 3) == m) for m in range(2)]

    def column(ref, r):
        parts = [jnp.where(here[m], ref[m, r : r + 1, :].astype(F32), 0.0) for m in range(2)]
        return jnp.sum(parts[0] + parts[1], axis=1, keepdims=True)

    spread = iota((16, 128), 0) == (iota((16, 128), 1) & 15)

    def along(col):
        return jnp.sum(jnp.where(spread, col, 0.0), axis=0, keepdims=True)

    cols = [column(route_ref, r) for r in range(2)]
    codes = [column(code_ref, r) for r in range(2)]
    whole = codes[0] + codes[1]
    lanes = jnp.concatenate([along(col) for col in cols], axis=0)
    share = jnp.concatenate([along(code / whole) for code in codes], axis=0)
    return jnp.concatenate(cols, axis=1), lanes, share


def slot_ranks(cols, lanes):
    width = lanes.shape[1]
    tok_col = iota((16, width), 0)
    tok_lane = iota((16, width), 1) & 15
    same = (tok_col >> 3) == (tok_lane >> 3)
    before = same & (tok_col < tok_lane)
    upto = same & (tok_col <= tok_lane)
    col0, col1 = cols[:, 0:1], cols[:, 1:2]
    lane0, lane1 = lanes[0:1, :], lanes[1:2, :]

    def count(mask):
        return jnp.sum(jnp.where(mask, 1.0, 0.0), axis=0, keepdims=True)

    rank0 = count((col0 == lane0) & before) + count((col1 == lane0) & before)
    rank1 = count((col0 == lane1) & upto) + count((col1 == lane1) & before)
    return rank0, rank1


def slot_masks(rows, shift, cols, lanes):
    width = lanes.shape[1]
    rank0, rank1 = slot_ranks(cols, lanes)
    row = iota((rows, width), 0)
    lane = iota((rows, width), 1)
    expert = (row >> shift).astype(F32)
    slot = (row & 1).astype(F32)
    fits = (((row >> 2) & 3) == ((lane >> 4) & 3)) & (((row >> 1) & 1) == ((lane >> 3) & 1))
    mask0 = fits & (lanes[0:1, :] == expert) & (rank0 == slot)
    mask1 = fits & (lanes[1:2, :] == expert) & (rank1 == slot)
    return mask0, mask1


def kernel(
    scale_factor,
    n_dp,
    n_peer,
    route_hbm,
    code_hbm,
    tok_hbm,
    cot_hbm,
    wg_hbm,
    wu_hbm,
    wd_hbm,
    mixed_ref,
    back_ref,
    gg_ref,
    gu_ref,
    gd_ref,
    route_ref,
    code_ref,
    tok_ref,
    cot_ref,
    wg,
    wu,
    wd,
    outbox,
    relay,
    inbox,
    xs,
    xt,
    xt_pair,
    gs,
    gs_pair,
    retbox,
    mate_near,
    mate_far,
    crossbox,
    colbox,
    retin,
    comb,
    parts,
    ring,
    zout,
    zbox,
    w_sem,
    xs_sem,
    xr_sem,
    ps_sem,
    os_sem,
    hs_sem,
    pr_sem,
    ms_sem,
    mr_sem,
    qs_sem,
    qr_sem,
    bs_sem,
    br_sem,
    cs_sem,
    cr_sem,
    ys_sem,
    yr_sem,
    zs_sem,
    zr_sem,
):
    k = lax.axis_index("expert")
    i = lax.axis_index("dp")
    n_y = n_dp // 4
    n_x = n_peer // 4
    x, z = k // 4, k % 4
    y, zh, core = i // 4, (i // 2) % 2, i % 2
    pair = y * 4 + zh * 2 + (1 - core)
    zpart = y * 4 + (1 - zh) * 2 + core
    up = ((y + 1) % n_y) * 4 + zh * 2 + core
    down = ((y + n_y - 1) % n_y) * 4 + zh * 2 + core

    loads = (
        (route_hbm, route_ref),
        (code_hbm, code_ref),
        (tok_hbm, tok_ref),
        (cot_hbm, cot_ref),
        (wg_hbm.at[0], wg),
        (wu_hbm.at[0], wu),
        (wd_hbm.at[0], wd),
    )
    loads = [pltpu.make_async_copy(src, dst, w_sem.at[n]) for n, (src, dst) in enumerate(loads)]
    t_copies, w_copies = loads[:4], loads[4:]
    for copy in loads:
        copy.start()

    barrier = pltpu.get_barrier_semaphore()

    for n in range(1, n_x):
        pl.semaphore_signal(
            barrier, inc=1, device_id={"expert": (x + n) % n_x * 4 + z}, device_id_type=MESH
        )
    for n in range(1, 4):
        pl.semaphore_signal(
            barrier, inc=1, device_id={"expert": x * 4 + (z + n) % 4}, device_id_type=MESH
        )
    for other in (pair, zpart, up, down):
        pl.semaphore_signal(barrier, inc=1, device_id={"dp": other}, device_id_type=MESH)

    for copy in t_copies:
        copy.wait()

    cols, all_lanes, all_share = route_vectors(route_ref, code_ref)
    lanes = all_lanes[:, 0:64]
    share = all_share[:, 0:64]
    mask0, mask1 = slot_masks(256, 4, cols, lanes)
    pick = jnp.where(mask0 | mask1, 1.0, 0.0).astype(BF16)
    slot_share = jnp.sum(
        jnp.where(mask0, share[0:1, :], 0.0) + jnp.where(mask1, share[1:2, :], 0.0),
        axis=1,
        keepdims=True,
    )
    is_cot = ((iota((256, 1), 0) >> 2) & 1) == 1
    slot_scale = jnp.where(is_cot, slot_share, 1.0)
    stack = jnp.concatenate(
        [
            ref[m, :, d * 1024 : (d + 1) * 1024]
            for d in range(2)
            for ref in (tok_ref, cot_ref)
            for m in range(2)
        ],
        axis=0,
    )
    outbox[...] = (slot_scale * dot(pick, stack)).astype(BF16).reshape(16, 16, 1024)

    pl.semaphore_wait(barrier, n_x - 1 + 3 + 4)

    def over_x(at):
        return pltpu.make_async_remote_copy(
            src_ref=outbox.at[pl.ds((x + ORDER[at]) % n_x * 2, 2)],
            dst_ref=relay.at[at],
            send_sem=xs_sem.at[at],
            recv_sem=xr_sem.at[at],
            device_id={"expert": (x + ORDER[at]) % n_x * 4 + z},
            device_id_type=MESH,
        )

    def to_pair(at):
        return pltpu.make_async_remote_copy(
            src_ref=relay.at[at, z // 2],
            dst_ref=inbox.at[at, z],
            send_sem=ps_sem.at[at],
            recv_sem=pr_sem.at[at, z],
            device_id={"expert": x * 4 + z + 1 - z % 2 * 2},
            device_id_type=MESH,
        )

    def to_other(at):
        return pltpu.make_async_remote_copy(
            src_ref=relay.at[at, 1 - z // 2],
            dst_ref=inbox.at[at, z],
            send_sem=os_sem.at[at],
            recv_sem=pr_sem.at[at, z],
            device_id={"expert": x * 4 + (1 - z // 2) * 2 + at % 2},
            device_id_type=MESH,
        )

    def hand_on(turn, b):
        at = turn * 2 + z % 2
        source = (1 - z // 2) * 2 + b
        return pltpu.make_async_remote_copy(
            src_ref=inbox.at[at, source],
            dst_ref=inbox.at[at, source],
            send_sem=hs_sem.at[turn, b],
            recv_sem=pr_sem.at[at, source],
            device_id={"expert": x * 4 + z + 1 - z % 2 * 2},
            device_id_type=MESH,
        )

    def arrival(at, source):
        return pltpu.make_async_remote_copy(
            src_ref=inbox.at[at, source],
            dst_ref=inbox.at[at, source],
            send_sem=ps_sem.at[0],
            recv_sem=pr_sem.at[at, source],
            device_id={"expert": x * 4 + z + 1 - z % 2 * 2},
            device_id_type=MESH,
        )

    for at in range(1, n_x):
        over_x(at).start()
    relay[0] = outbox[pl.ds(x * 2, 2)]

    lane = iota((2, 128), 1)
    weight = jnp.where(((lane >> 4) & 1) == 0, all_share, 1.0)
    high = weight.astype(BF16).astype(F32)
    weight = jnp.where(lane < 64, high, weight - high)
    mask0, mask1 = slot_masks(256, 4, cols, all_lanes)
    comb[...] = (
        jnp.where(mask0, weight[0:1, :], 0.0) + jnp.where(mask1, weight[1:2, :], 0.0)
    ).astype(BF16)

    row = iota((128, 128), 0)
    lane = iota((128, 128), 1)
    order = jnp.where(((row >> 2) & 7) * 16 + (row >> 5) * 4 + (row & 3) == lane, 1.0, 0.0)
    order = order.astype(BF16)

    def forward(at):
        if at:
            over_x(at).wait_recv()
        to_pair(at).start()
        to_other(at).start()
        inbox[at, z] = relay[at, z // 2]

    def relay_turn(turn):
        for b in range(2):
            arrival(turn * 2 + z % 2, (1 - z // 2) * 2 + b).wait_recv()
            hand_on(turn, b).start()

    def sort_rows(g):
        for at in (2 * g, 2 * g + 1):
            arrival(at, z + 1 - z % 2 * 2).wait_recv()
        for b in range(2):
            arrival(2 * g + 1 - z % 2, (1 - z // 2) * 2 + b).wait_recv()
        block = inbox[2 * g : 2 * g + 2].reshape(128, 1024)
        sorted_rows = dot(order, block).astype(BF16)
        for q in range(4):
            xs[q, g * 32 : (g + 1) * 32] = sorted_rows[q * 32 : (q + 1) * 32]

    forward(0)
    forward(1)
    forward(2)
    relay_turn(0)
    forward(3)
    forward(4)
    relay_turn(1)
    forward(5)
    forward(6)
    relay_turn(2)
    sort_rows(0)
    forward(7)
    sort_rows(1)
    relay_turn(3)
    sort_rows(2)
    sort_rows(3)

    for q in range(4):
        turned = jnp.transpose(xs[q])
        xt[q % 2, (q // 2) * 8 : (q // 2 + 1) * 8] = turned.reshape(8, 2, 64, 128)
    xt_copy = pltpu.make_async_remote_copy(
        src_ref=xt.at[:, :, 1 - core],
        dst_ref=xt_pair,
        send_sem=cs_sem.at[0],
        recv_sem=cr_sem.at[0],
        device_id={"dp": pair},
        device_id_type=MESH,
    )
    xt_copy.start()

    for copy in w_copies:
        copy.wait()

    pre_gate = dot(xs[0], wg[0:1024]) + dot(xs[2], wg[1024:2048])
    pre_up = dot(xs[0], wu[0:1024]) + dot(xs[2], wu[1024:2048])
    grad_hidden = dot(xs[1], wd[0:1024]) + dot(xs[3], wd[1024:2048])
    sigma = jax.nn.sigmoid(pre_gate)
    activ = pre_gate * sigma
    hidden = (activ * pre_up).astype(BF16)
    grad_gate = (grad_hidden * pre_up * sigma * (1.0 + pre_gate * (1.0 - sigma))).astype(BF16)
    grad_up = (grad_hidden * activ).astype(BF16)
    gs[0] = grad_gate
    gs[1] = grad_up
    gs[2] = hidden
    gs_copy = pltpu.make_async_remote_copy(
        src_ref=gs,
        dst_ref=gs_pair,
        send_sem=cs_sem.at[1],
        recv_sem=cr_sem.at[1],
        device_id={"dp": pair},
        device_id_type=MESH,
    )
    gs_copy.start()

    def outputs(d):
        half = slice(d * 1024, (d + 1) * 1024)
        xs[2 * d] = dot_last(hidden, wd[half]).astype(BF16)
        xs[2 * d + 1] = (dot_last(grad_gate, wg[half]) + dot_last(grad_up, wu[half])).astype(BF16)

    outputs(0)

    xt_copy.wait_recv()
    gs_copy.wait_recv()

    def make_parts(*steps):
        pairs = [pl.ds((y + step) % n_y * 2, 2) for step in steps]
        for n in range(3):
            a = 0 if n < 2 else 1
            left = [
                jnp.concatenate(
                    [xt[a, two, core].reshape(128, 128), xt_pair[a, two].reshape(128, 128)], axis=1
                )
                for two in pairs
            ]
            right = jnp.concatenate([gs[n], gs_pair[n]], axis=0)
            part = (dot(jnp.concatenate(left, axis=0), right) * scale_factor).astype(BF16)
            for m, two in enumerate(pairs):
                rows = part[m * 128 : (m + 1) * 128].reshape(2, 64, part.shape[1])
                parts[two, n * 64 : (n + 1) * 64] = rows

    ways = [(half, d) for half in range(2) for d in range(2)]

    def hops(half, d):
        return n_y // 2 if half == d else (n_y - 1) // 2

    def own_piece(part, half, step):
        at = (y + step) % n_y * 2 + (1 - zh if part == 0 else zh)
        return parts.at[at, pl.ds(half * 96, 96)]

    def ring_copy(part, half, d, step, source=None):
        slot = ring.at[part, half, d, step]
        return pltpu.make_async_remote_copy(
            src_ref=slot if source is None else source,
            dst_ref=slot,
            send_sem=ys_sem.at[part, half, d, step],
            recv_sem=yr_sem.at[part, half, d, step],
            device_id={"dp": up if d == 0 else down},
            device_id_type=MESH,
        )

    def ring_send(part, step):
        for half, d in ways:
            left = hops(half, d) - step
            if left > 0:
                source = own_piece(part, half, left if d == 0 else n_y - left)
                if step:
                    ring_copy(part, half, d, step - 1).wait_recv()
                    total = ring[part, half, d, step - 1].astype(F32) + source[...].astype(F32)
                    ring[part, half, d, step - 1] = total.astype(BF16)
                    source = ring.at[part, half, d, step - 1]
                ring_copy(part, half, d, step, source).start()

    def ring_total(part, half):
        total = own_piece(part, half, 0)[...].astype(F32)
        for d in range(2):
            ring_copy(part, half, d, hops(half, d) - 1).wait_recv()
            total = total + ring[part, half, d, hops(half, d) - 1].astype(F32)
        return total

    make_parts(4, 3, n_y - 3)
    ring_send(0, 0)

    make_parts(2, n_y - 2)
    outputs(1)
    back_order = jnp.where(((lane >> 2) & 7) * 16 + (lane >> 5) * 4 + (lane & 3) == row, 1.0, 0.0)
    back_order = back_order.astype(BF16)
    for g in range(n_peer // 8):
        block = jnp.concatenate([xs[q, g * 32 : (g + 1) * 32] for q in range(4)], axis=0)
        retbox[2 * g : 2 * g + 2] = dot(back_order, block).astype(BF16).reshape(2, 4, 16, 1024)

    side, odd = z // 2, z % 2
    far = (1 - side) * 2
    mate = {"expert": x * 4 + z + 1 - odd * 2}

    def mate_own(turn):
        return pltpu.make_async_remote_copy(
            src_ref=retbox.at[pl.ds(2 * turn, 2), z + 1 - odd * 2],
            dst_ref=mate_near.at[turn],
            send_sem=ms_sem.at[turn, 0],
            recv_sem=mr_sem.at[turn, 0],
            device_id=mate,
            device_id_type=MESH,
        )

    def mate_other(turn):
        return pltpu.make_async_remote_copy(
            src_ref=retbox.at[2 * turn + 1 - odd, pl.ds(far, 2)],
            dst_ref=mate_far.at[turn],
            send_sem=ms_sem.at[turn, 1],
            recv_sem=mr_sem.at[turn, 1],
            device_id=mate,
            device_id_type=MESH,
        )

    def cross(turn, b):
        return pltpu.make_async_remote_copy(
            src_ref=crossbox.at[turn, b],
            dst_ref=colbox.at[2 * turn + odd, side],
            send_sem=qs_sem.at[turn, b],
            recv_sem=qr_sem.at[2 * turn + odd],
            device_id={"expert": x * 4 + far + b},
            device_id_type=MESH,
        )

    def cross_arrival(at):
        return pltpu.make_async_remote_copy(
            src_ref=colbox.at[at, 1 - side],
            dst_ref=colbox.at[at, 1 - side],
            send_sem=qs_sem.at[0, 0],
            recv_sem=qr_sem.at[at],
            device_id=mate,
            device_id_type=MESH,
        )

    def home(at):
        return pltpu.make_async_remote_copy(
            src_ref=colbox.at[at],
            dst_ref=retin.at[pl.ds(x * 2, 2)],
            send_sem=bs_sem.at[at],
            recv_sem=br_sem.at[at],
            device_id={"expert": (x + n_x - ORDER[at]) % n_x * 4 + z},
            device_id_type=MESH,
        )

    def home_arrival(at):
        return pltpu.make_async_remote_copy(
            src_ref=colbox.at[at],
            dst_ref=retin.at[pl.ds((x + ORDER[at]) % n_x * 2, 2)],
            send_sem=bs_sem.at[at],
            recv_sem=br_sem.at[at],
            device_id=mate,
            device_id_type=MESH,
        )

    def sum_turn(turn):
        mate_own(turn).wait_recv()
        mate_other(turn).wait_recv()
        two = pl.ds(2 * turn, 2)
        colbox[two, side] = (retbox[two, z].astype(F32) + mate_near[turn].astype(F32)).astype(BF16)
        crossbox[turn] = (
            retbox[2 * turn + odd, pl.ds(far, 2)].astype(F32) + mate_far[turn].astype(F32)
        ).astype(BF16)
        for b in range(2):
            cross(turn, b).start()

    def home_turn(turn):
        for at in (2 * turn + 1, 2 * turn):
            cross_arrival(at).wait_recv()
            if at:
                home(at).start()
            else:
                retin[pl.ds(x * 2, 2)] = colbox[0]

    for turn in (3, 2, 1, 0):
        mate_other(turn).start()
        mate_own(turn).start()

    z_copies = [
        pltpu.make_async_remote_copy(
            src_ref=zout.at[half],
            dst_ref=zbox.at[half],
            send_sem=zs_sem.at[half],
            recv_sem=zr_sem.at[half],
            device_id={"dp": zpart},
            device_id_type=MESH,
        )
        for half in range(2)
    ]
    ring_send(0, 1)
    ring_send(1, 0)
    make_parts(1, n_y - 1, 0)
    sum_turn(3)
    ring_send(0, 2)
    ring_send(1, 1)
    sum_turn(2)
    home_turn(3)
    sum_turn(1)
    home_turn(2)
    ring_send(0, 3)
    ring_send(1, 2)
    sum_turn(0)
    home_turn(1)
    for half in range(2):
        zout[half] = ring_total(0, half).astype(BF16)
        z_copies[half].start()
    ring_send(1, 3)

    home_turn(0)
    for at in range(n_x - 1, 0, -1):
        home_arrival(at).wait_recv()
    both = dot_first(comb[...], retin[...].reshape(256, 1024))
    total = (both[0:64] + both[64:128]).astype(BF16)
    for m in range(2):
        for d in range(2):
            half = slice(d * 1024, (d + 1) * 1024)
            at = d * 32 + m * 8
            mixed_ref[m, :, half] = total[at : at + 8]
            back_ref[m, :, half] = total[at + 16 : at + 24]

    sums = []
    for half in range(2):
        total = ring_total(1, half)
        z_copies[half].wait_recv()
        sums.append(total + zbox[half].astype(F32))
    gg_ref[0] = sums[0][0:64]
    gu_ref[0, 0:32] = sums[0][64:96]
    gu_ref[0, 32:64] = sums[1][0:32]
    gd_ref[0] = sums[1][32:96]

    for at in range(n_x):
        if at:
            over_x(at).wait_send()
        to_pair(at).wait_send()
        to_other(at).wait_send()
    for turn in range(n_x // 2):
        for b in range(2):
            hand_on(turn, b).wait_send()
    for turn in range(n_x // 2):
        mate_own(turn).wait_send()
        mate_other(turn).wait_send()
        for b in range(2):
            cross(turn, b).wait_send()
    for at in range(1, n_x):
        home(at).wait_send()
    xt_copy.wait_send()
    gs_copy.wait_send()

    for part in range(2):
        for half, d in ways:
            for step in range(hops(half, d)):
                ring_copy(part, half, d, step).wait_send()
    for copy in z_copies:
        copy.wait_send()


def write_kernel(count, *refs):
    ins, outs, held = refs[:count], refs[count : 2 * count], refs[2 * count : 3 * count]
    in_sem, out_sem = refs[3 * count :]
    reads = [pltpu.make_async_copy(ins[n], held[n], in_sem.at[n]) for n in range(count)]
    writes = [pltpu.make_async_copy(held[n], outs[n], out_sem.at[n]) for n in range(count)]
    for copy in reads:
        copy.start()
    for n in range(count):
        reads[n].wait()
        writes[n].start()
    for copy in writes:
        copy.wait()


def shards(tokens, cotangent, routes, gate_codes, gate_weight, up_weight, down_weight):
    micro, toks, width = tokens.shape
    n_peer = lax.axis_size("expert")
    n_dp = lax.axis_size("dp")
    hidden = gate_weight.shape[2]
    scale_factor = 1.0 / math.sqrt(n_dp * micro * n_peer * 2)
    n_y = n_dp // 4
    n_x = n_peer // 4
    vmem = pl.BlockSpec(memory_space=pltpu.VMEM)
    hbm = pl.BlockSpec(memory_space=pltpu.HBM)
    anyspace = pl.BlockSpec(memory_space=pl.ANY)
    dma = pltpu.SemaphoreType.DMA
    tok = jax.ShapeDtypeStruct((micro, toks, width), BF16)
    grad = jax.ShapeDtypeStruct((1, width // n_dp, hidden), F32)
    shapes = (tok, tok, grad, grad, grad)
    results = pl.pallas_call(
        functools.partial(kernel, scale_factor, n_dp, n_peer),
        out_shape=shapes,
        in_specs=[hbm] * 7,
        out_specs=(vmem,) * 5,
        scratch_shapes=[
            pltpu.VMEM((micro, 2, toks), jnp.int32),
            pltpu.VMEM((micro, 2, toks), jnp.int32),
            pltpu.VMEM((micro, toks, width), BF16),
            pltpu.VMEM((micro, toks, width), BF16),
            pltpu.VMEM((width, hidden), BF16),
            pltpu.VMEM((width, hidden), BF16),
            pltpu.VMEM((width, hidden), BF16),
            pltpu.VMEM((n_peer // 2, 16, 1024), BF16),
            pltpu.VMEM((n_x, 2, 16, 1024), BF16),
            pltpu.VMEM((n_x, 4, 16, 1024), BF16),
            pltpu.VMEM((4, 128, 1024), BF16),
            pltpu.VMEM((2, 16, 2, 64, 128), BF16),
            pltpu.VMEM((2, 16, 64, 128), BF16),
            pltpu.VMEM((3, 128, hidden), BF16),
            pltpu.VMEM((3, 128, hidden), BF16),
            pltpu.VMEM((n_x, 4, 16, 1024), BF16),
            pltpu.VMEM((n_x // 2, 2, 16, 1024), BF16),
            pltpu.VMEM((n_x // 2, 2, 16, 1024), BF16),
            pltpu.VMEM((n_x // 2, 2, 16, 1024), BF16),
            pltpu.VMEM((n_x, 2, 16, 1024), BF16),
            pltpu.VMEM((n_peer // 2, 16, 1024), BF16),
            pltpu.VMEM((256, 128), BF16),
            pltpu.VMEM((16, 192, hidden), BF16),
            pltpu.VMEM((2, 2, 2, n_y // 2, 96, hidden), BF16),
            pltpu.VMEM((2, 96, hidden), BF16),
            pltpu.VMEM((2, 96, hidden), BF16),
            dma((7,)),
            dma((n_x,)),
            dma((n_x,)),
            dma((n_x,)),
            dma((n_x,)),
            dma((n_x // 2, 2)),
            dma((n_x, 4)),
            dma((n_x // 2, 2)),
            dma((n_x // 2, 2)),
            dma((n_x // 2, 2)),
            dma((n_x,)),
            dma((n_x,)),
            dma((n_x,)),
            dma((2,)),
            dma((2,)),
            dma((2, 2, 2, n_y // 2)),
            dma((2, 2, 2, n_y // 2)),
            dma((2,)),
            dma((2,)),
        ],
        compiler_params=pltpu.CompilerParams(
            collective_id=0, has_side_effects=True, vmem_limit_bytes=56 * 1024 * 1024
        ),
        name="moe_layer",
    )(
        routes.transpose(0, 2, 1),
        gate_codes.transpose(0, 2, 1),
        tokens,
        cotangent,
        gate_weight,
        up_weight,
        down_weight,
    )
    return pl.pallas_call(
        functools.partial(write_kernel, len(shapes)),
        out_shape=shapes,
        in_specs=[anyspace] * len(shapes),
        out_specs=(hbm,) * len(shapes),
        scratch_shapes=[pltpu.VMEM(one.shape, one.dtype) for one in shapes]
        + [dma((len(shapes),)), dma((len(shapes),))],
        name="write_out",
    )(*results)


def solution(mesh):
    tok_spec = P(None, ("dp", "expert"), None)
    w_spec = P("expert", None, None)
    g_spec = P("expert", "dp", None)
    return jax.shard_map(
        shards,
        mesh=mesh,
        in_specs=(tok_spec,) * 4 + (w_spec,) * 3,
        out_specs=(tok_spec,) * 2 + (g_spec,) * 3,
        check_vma=False,
    )
```

```python
import functools
import math

import jax
import jax.numpy as jnp
from jax import lax
from jax.experimental import pallas as pl
from jax.experimental.pallas import tpu as pltpu
from jax.sharding import PartitionSpec as P

MESH = pl.DeviceIdType.MESH
F32 = jnp.float32
BF16 = jnp.bfloat16

ORDER = (0, 1, 7, 2, 6, 3, 5, 4)


def dot(left, right):
    return jnp.dot(left, right, preferred_element_type=F32)


def dot_last(left, right):
    return lax.dot_general(left, right, (((1,), (1,)), ((), ())), preferred_element_type=F32)


def dot_first(left, right):
    return lax.dot_general(left, right, (((0,), (0,)), ((), ())), preferred_element_type=F32)


def iota(shape, axis):
    return lax.broadcasted_iota(jnp.int32, shape, axis)


def route_vectors(route_ref, code_ref):
    row = iota((16, 8), 0)
    lane = iota((16, 8), 1)
    here = [(lane == (row & 7)) & ((row >> 3) == m) for m in range(2)]

    def column(ref, r):
        parts = [jnp.where(here[m], ref[m, r : r + 1, :].astype(F32), 0.0) for m in range(2)]
        return jnp.sum(parts[0] + parts[1], axis=1, keepdims=True)

    spread = iota((16, 128), 0) == (iota((16, 128), 1) & 15)

    def along(col):
        return jnp.sum(jnp.where(spread, col, 0.0), axis=0, keepdims=True)

    cols = [column(route_ref, r) for r in range(2)]
    codes = [column(code_ref, r) for r in range(2)]
    whole = codes[0] + codes[1]
    lanes = jnp.concatenate([along(col) for col in cols], axis=0)
    share = jnp.concatenate([along(code / whole) for code in codes], axis=0)
    return jnp.concatenate(cols, axis=1), lanes, share


def slot_ranks(cols, lanes):
    width = lanes.shape[1]
    tok_col = iota((16, width), 0)
    tok_lane = iota((16, width), 1) & 15
    same = (tok_col >> 3) == (tok_lane >> 3)
    before = same & (tok_col < tok_lane)
    upto = same & (tok_col <= tok_lane)
    col0, col1 = cols[:, 0:1], cols[:, 1:2]
    lane0, lane1 = lanes[0:1, :], lanes[1:2, :]

    def count(mask):
        return jnp.sum(jnp.where(mask, 1.0, 0.0), axis=0, keepdims=True)

    rank0 = count((col0 == lane0) & before) + count((col1 == lane0) & before)
    rank1 = count((col0 == lane1) & upto) + count((col1 == lane1) & before)
    return rank0, rank1


def slot_masks(rows, shift, cols, lanes):
    width = lanes.shape[1]
    rank0, rank1 = slot_ranks(cols, lanes)
    row = iota((rows, width), 0)
    lane = iota((rows, width), 1)
    expert = (row >> shift).astype(F32)
    slot = (row & 1).astype(F32)
    fits = (((row >> 2) & 3) == ((lane >> 4) & 3)) & (((row >> 1) & 1) == ((lane >> 3) & 1))
    mask0 = fits & (lanes[0:1, :] == expert) & (rank0 == slot)
    mask1 = fits & (lanes[1:2, :] == expert) & (rank1 == slot)
    return mask0, mask1


def kernel(
    scale_factor,
    n_dp,
    n_peer,
    route_hbm,
    code_hbm,
    tok_hbm,
    cot_hbm,
    wg_hbm,
    wu_hbm,
    wd_hbm,
    mixed_ref,
    back_ref,
    gg_ref,
    gu_ref,
    gd_ref,
    route_ref,
    code_ref,
    tok_ref,
    cot_ref,
    wg,
    wu,
    wd,
    outbox,
    relay,
    inbox,
    xs,
    xt,
    xt_pair,
    gs,
    gs_pair,
    retbox,
    mate_near,
    mate_far,
    crossbox,
    colbox,
    retin,
    comb,
    parts,
    ring,
    zout,
    zbox,
    w_sem,
    xs_sem,
    xr_sem,
    ps_sem,
    os_sem,
    hs_sem,
    pr_sem,
    ms_sem,
    mr_sem,
    qs_sem,
    qr_sem,
    bs_sem,
    br_sem,
    cs_sem,
    cr_sem,
    ys_sem,
    yr_sem,
    zs_sem,
    zr_sem,
):
    k = lax.axis_index("expert")
    i = lax.axis_index("dp")
    n_y = n_dp // 4
    n_x = n_peer // 4
    x, z = k // 4, k % 4
    y, zh, core = i // 4, (i // 2) % 2, i % 2
    pair = y * 4 + zh * 2 + (1 - core)
    zpart = y * 4 + (1 - zh) * 2 + core
    up = ((y + 1) % n_y) * 4 + zh * 2 + core
    down = ((y + n_y - 1) % n_y) * 4 + zh * 2 + core

    loads = (
        (route_hbm, route_ref),
        (code_hbm, code_ref),
        (tok_hbm, tok_ref),
        (cot_hbm, cot_ref),
        (wg_hbm.at[0], wg),
        (wu_hbm.at[0], wu),
        (wd_hbm.at[0], wd),
    )
    loads = [pltpu.make_async_copy(src, dst, w_sem.at[n]) for n, (src, dst) in enumerate(loads)]
    t_copies, w_copies = loads[:4], loads[4:]
    for copy in loads:
        copy.start()

    barrier = pltpu.get_barrier_semaphore()

    for n in range(1, n_x):
        pl.semaphore_signal(
            barrier, inc=1, device_id={"expert": (x + n) % n_x * 4 + z}, device_id_type=MESH
        )
    for n in range(1, 4):
        pl.semaphore_signal(
            barrier, inc=1, device_id={"expert": x * 4 + (z + n) % 4}, device_id_type=MESH
        )
    for other in (pair, zpart, up, down):
        pl.semaphore_signal(barrier, inc=1, device_id={"dp": other}, device_id_type=MESH)

    for copy in t_copies:
        copy.wait()

    cols, all_lanes, all_share = route_vectors(route_ref, code_ref)
    lanes = all_lanes[:, 0:64]
    share = all_share[:, 0:64]
    mask0, mask1 = slot_masks(256, 4, cols, lanes)
    pick = jnp.where(mask0 | mask1, 1.0, 0.0).astype(BF16)
    slot_share = jnp.sum(
        jnp.where(mask0, share[0:1, :], 0.0) + jnp.where(mask1, share[1:2, :], 0.0),
        axis=1,
        keepdims=True,
    )
    is_cot = ((iota((256, 1), 0) >> 2) & 1) == 1
    slot_scale = jnp.where(is_cot, slot_share, 1.0)
    stack = jnp.concatenate(
        [
            ref[m, :, d * 1024 : (d + 1) * 1024]
            for d in range(2)
            for ref in (tok_ref, cot_ref)
            for m in range(2)
        ],
        axis=0,
    )
    outbox[...] = (slot_scale * dot(pick, stack)).astype(BF16).reshape(16, 16, 1024)

    pl.semaphore_wait(barrier, n_x - 1 + 3 + 4)

    def over_x(at):
        return pltpu.make_async_remote_copy(
            src_ref=outbox.at[pl.ds((x + ORDER[at]) % n_x * 2, 2)],
            dst_ref=relay.at[at],
            send_sem=xs_sem.at[at],
            recv_sem=xr_sem.at[at],
            device_id={"expert": (x + ORDER[at]) % n_x * 4 + z},
            device_id_type=MESH,
        )

    def to_pair(at):
        return pltpu.make_async_remote_copy(
            src_ref=relay.at[at, z // 2],
            dst_ref=inbox.at[at, z],
            send_sem=ps_sem.at[at],
            recv_sem=pr_sem.at[at, z],
            device_id={"expert": x * 4 + z + 1 - z % 2 * 2},
            device_id_type=MESH,
        )

    def to_other(at):
        return pltpu.make_async_remote_copy(
            src_ref=relay.at[at, 1 - z // 2],
            dst_ref=inbox.at[at, z],
            send_sem=os_sem.at[at],
            recv_sem=pr_sem.at[at, z],
            device_id={"expert": x * 4 + (1 - z // 2) * 2 + at % 2},
            device_id_type=MESH,
        )

    def hand_on(turn, b):
        at = turn * 2 + z % 2
        source = (1 - z // 2) * 2 + b
        return pltpu.make_async_remote_copy(
            src_ref=inbox.at[at, source],
            dst_ref=inbox.at[at, source],
            send_sem=hs_sem.at[turn, b],
            recv_sem=pr_sem.at[at, source],
            device_id={"expert": x * 4 + z + 1 - z % 2 * 2},
            device_id_type=MESH,
        )

    def arrival(at, source):
        return pltpu.make_async_remote_copy(
            src_ref=inbox.at[at, source],
            dst_ref=inbox.at[at, source],
            send_sem=ps_sem.at[0],
            recv_sem=pr_sem.at[at, source],
            device_id={"expert": x * 4 + z + 1 - z % 2 * 2},
            device_id_type=MESH,
        )

    for at in range(1, n_x):
        over_x(at).start()
    relay[0] = outbox[pl.ds(x * 2, 2)]

    lane = iota((2, 128), 1)
    weight = jnp.where(((lane >> 4) & 1) == 0, all_share, 1.0)
    high = weight.astype(BF16).astype(F32)
    weight = jnp.where(lane < 64, high, weight - high)
    mask0, mask1 = slot_masks(256, 4, cols, all_lanes)
    comb[...] = (
        jnp.where(mask0, weight[0:1, :], 0.0) + jnp.where(mask1, weight[1:2, :], 0.0)
    ).astype(BF16)

    row = iota((128, 128), 0)
    lane = iota((128, 128), 1)
    order = jnp.where(((row >> 2) & 7) * 16 + (row >> 5) * 4 + (row & 3) == lane, 1.0, 0.0)
    order = order.astype(BF16)

    def forward(at):
        if at:
            over_x(at).wait_recv()
        to_other(at).start()
        to_pair(at).start()
        inbox[at, z] = relay[at, z // 2]

    def relay_turn(turn):
        for b in range(2):
            arrival(turn * 2 + z % 2, (1 - z // 2) * 2 + b).wait_recv()
            hand_on(turn, b).start()

    def sort_rows(g):
        for at in (2 * g, 2 * g + 1):
            arrival(at, z + 1 - z % 2 * 2).wait_recv()
        for b in range(2):
            arrival(2 * g + 1 - z % 2, (1 - z // 2) * 2 + b).wait_recv()
        block = inbox[2 * g : 2 * g + 2].reshape(128, 1024)
        sorted_rows = dot(order, block).astype(BF16)
        for q in range(4):
            xs[q, g * 32 : (g + 1) * 32] = sorted_rows[q * 32 : (q + 1) * 32]

    forward(0)
    forward(1)
    forward(2)
    relay_turn(0)
    forward(3)
    forward(4)
    relay_turn(1)
    forward(5)
    forward(6)
    sort_rows(0)
    forward(7)
    relay_turn(2)
    sort_rows(1)
    relay_turn(3)
    sort_rows(2)
    sort_rows(3)

    for q in range(4):
        turned = jnp.transpose(xs[q])
        xt[q % 2, (q // 2) * 8 : (q // 2 + 1) * 8] = turned.reshape(8, 2, 64, 128)
    xt_copy = pltpu.make_async_remote_copy(
        src_ref=xt.at[:, :, 1 - core],
        dst_ref=xt_pair,
        send_sem=cs_sem.at[0],
        recv_sem=cr_sem.at[0],
        device_id={"dp": pair},
        device_id_type=MESH,
    )
    xt_copy.start()

    for copy in w_copies:
        copy.wait()

    pre_gate = dot(xs[0], wg[0:1024]) + dot(xs[2], wg[1024:2048])
    pre_up = dot(xs[0], wu[0:1024]) + dot(xs[2], wu[1024:2048])
    grad_hidden = dot(xs[1], wd[0:1024]) + dot(xs[3], wd[1024:2048])
    sigma = jax.nn.sigmoid(pre_gate)
    activ = pre_gate * sigma
    hidden = (activ * pre_up).astype(BF16)
    grad_gate = (grad_hidden * pre_up * sigma * (1.0 + pre_gate * (1.0 - sigma))).astype(BF16)
    grad_up = (grad_hidden * activ).astype(BF16)
    gs[0] = grad_gate
    gs[1] = grad_up
    gs[2] = hidden
    gs_copy = pltpu.make_async_remote_copy(
        src_ref=gs,
        dst_ref=gs_pair,
        send_sem=cs_sem.at[1],
        recv_sem=cr_sem.at[1],
        device_id={"dp": pair},
        device_id_type=MESH,
    )
    gs_copy.start()

    def outputs(d):
        half = slice(d * 1024, (d + 1) * 1024)
        xs[2 * d] = dot_last(hidden, wd[half]).astype(BF16)
        xs[2 * d + 1] = (dot_last(grad_gate, wg[half]) + dot_last(grad_up, wu[half])).astype(BF16)


    xt_copy.wait_recv()
    gs_copy.wait_recv()

    def make_parts(*steps):
        pairs = [pl.ds((y + step) % n_y * 2, 2) for step in steps]
        for n in range(3):
            a = 0 if n < 2 else 1
            left = [
                jnp.concatenate(
                    [xt[a, two, core].reshape(128, 128), xt_pair[a, two].reshape(128, 128)], axis=1
                )
                for two in pairs
            ]
            right = jnp.concatenate([gs[n], gs_pair[n]], axis=0)
            part = (dot(jnp.concatenate(left, axis=0), right) * scale_factor).astype(BF16)
            for m, two in enumerate(pairs):
                rows = part[m * 128 : (m + 1) * 128].reshape(2, 64, part.shape[1])
                parts[two, n * 64 : (n + 1) * 64] = rows

    ways = [(half, d) for half in range(2) for d in range(2)]

    def hops(half, d):
        return n_y // 2 if half == d else (n_y - 1) // 2

    def own_piece(part, half, step):
        at = (y + step) % n_y * 2 + (1 - zh if part == 0 else zh)
        return parts.at[at, pl.ds(half * 96, 96)]

    def ring_copy(part, half, d, step, source=None):
        slot = ring.at[part, half, d, step]
        return pltpu.make_async_remote_copy(
            src_ref=slot if source is None else source,
            dst_ref=slot,
            send_sem=ys_sem.at[part, half, d, step],
            recv_sem=yr_sem.at[part, half, d, step],
            device_id={"dp": up if d == 0 else down},
            device_id_type=MESH,
        )

    def ring_send(part, step):
        for half, d in ways:
            left = hops(half, d) - step
            if left > 0:
                source = own_piece(part, half, left if d == 0 else n_y - left)
                if step:
                    ring_copy(part, half, d, step - 1).wait_recv()
                    total = ring[part, half, d, step - 1].astype(F32) + source[...].astype(F32)
                    ring[part, half, d, step - 1] = total.astype(BF16)
                    source = ring.at[part, half, d, step - 1]
                ring_copy(part, half, d, step, source).start()

    def ring_total(part, half):
        total = own_piece(part, half, 0)[...].astype(F32)
        for d in range(2):
            ring_copy(part, half, d, hops(half, d) - 1).wait_recv()
            total = total + ring[part, half, d, hops(half, d) - 1].astype(F32)
        return total

    make_parts(4, 3, n_y - 3)
    ring_send(0, 0)

    outputs(0)
    make_parts(2, n_y - 2)
    outputs(1)
    back_order = jnp.where(((lane >> 2) & 7) * 16 + (lane >> 5) * 4 + (lane & 3) == row, 1.0, 0.0)
    back_order = back_order.astype(BF16)
    for g in range(n_peer // 8):
        block = jnp.concatenate([xs[q, g * 32 : (g + 1) * 32] for q in range(4)], axis=0)
        retbox[2 * g : 2 * g + 2] = dot(back_order, block).astype(BF16).reshape(2, 4, 16, 1024)

    side, odd = z // 2, z % 2
    far = (1 - side) * 2
    mate = {"expert": x * 4 + z + 1 - odd * 2}

    def mate_own(turn):
        return pltpu.make_async_remote_copy(
            src_ref=retbox.at[pl.ds(2 * turn, 2), z + 1 - odd * 2],
            dst_ref=mate_near.at[turn],
            send_sem=ms_sem.at[turn, 0],
            recv_sem=mr_sem.at[turn, 0],
            device_id=mate,
            device_id_type=MESH,
        )

    def mate_other(turn):
        return pltpu.make_async_remote_copy(
            src_ref=retbox.at[2 * turn + 1 - odd, pl.ds(far, 2)],
            dst_ref=mate_far.at[turn],
            send_sem=ms_sem.at[turn, 1],
            recv_sem=mr_sem.at[turn, 1],
            device_id=mate,
            device_id_type=MESH,
        )

    def cross(turn, b):
        return pltpu.make_async_remote_copy(
            src_ref=crossbox.at[turn, b],
            dst_ref=colbox.at[2 * turn + odd, side],
            send_sem=qs_sem.at[turn, b],
            recv_sem=qr_sem.at[2 * turn + odd],
            device_id={"expert": x * 4 + far + b},
            device_id_type=MESH,
        )

    def cross_arrival(at):
        return pltpu.make_async_remote_copy(
            src_ref=colbox.at[at, 1 - side],
            dst_ref=colbox.at[at, 1 - side],
            send_sem=qs_sem.at[0, 0],
            recv_sem=qr_sem.at[at],
            device_id=mate,
            device_id_type=MESH,
        )

    def home(at):
        return pltpu.make_async_remote_copy(
            src_ref=colbox.at[at],
            dst_ref=retin.at[pl.ds(x * 2, 2)],
            send_sem=bs_sem.at[at],
            recv_sem=br_sem.at[at],
            device_id={"expert": (x + n_x - ORDER[at]) % n_x * 4 + z},
            device_id_type=MESH,
        )

    def home_arrival(at):
        return pltpu.make_async_remote_copy(
            src_ref=colbox.at[at],
            dst_ref=retin.at[pl.ds((x + ORDER[at]) % n_x * 2, 2)],
            send_sem=bs_sem.at[at],
            recv_sem=br_sem.at[at],
            device_id=mate,
            device_id_type=MESH,
        )

    def sum_turn(turn):
        mate_own(turn).wait_recv()
        mate_other(turn).wait_recv()
        two = pl.ds(2 * turn, 2)
        colbox[two, side] = (retbox[two, z].astype(F32) + mate_near[turn].astype(F32)).astype(BF16)
        crossbox[turn] = (
            retbox[2 * turn + odd, pl.ds(far, 2)].astype(F32) + mate_far[turn].astype(F32)
        ).astype(BF16)
        for b in range(2):
            cross(turn, b).start()

    def home_turn(turn):
        for at in (2 * turn + 1, 2 * turn):
            cross_arrival(at).wait_recv()
            if at:
                home(at).start()
            else:
                retin[pl.ds(x * 2, 2)] = colbox[0]

    for turn in (3, 2, 1, 0):
        mate_other(turn).start()
        mate_own(turn).start()

    z_copies = [
        pltpu.make_async_remote_copy(
            src_ref=zout.at[half],
            dst_ref=zbox.at[half],
            send_sem=zs_sem.at[half],
            recv_sem=zr_sem.at[half],
            device_id={"dp": zpart},
            device_id_type=MESH,
        )
        for half in range(2)
    ]
    ring_send(0, 1)
    ring_send(1, 0)
    make_parts(1, n_y - 1, 0)
    sum_turn(3)
    ring_send(0, 2)
    ring_send(1, 1)
    sum_turn(2)
    home_turn(3)
    sum_turn(1)
    home_turn(2)
    ring_send(0, 3)
    ring_send(1, 2)
    sum_turn(0)
    home_turn(1)
    for half in range(2):
        zout[half] = ring_total(0, half).astype(BF16)
        z_copies[half].start()
    ring_send(1, 3)

    home_turn(0)
    for at in range(n_x - 1, 0, -1):
        home_arrival(at).wait_recv()
    both = dot_first(comb[...], retin[...].reshape(256, 1024))
    total = (both[0:64] + both[64:128]).astype(BF16)
    for m in range(2):
        for d in range(2):
            half = slice(d * 1024, (d + 1) * 1024)
            at = d * 32 + m * 8
            mixed_ref[m, :, half] = total[at : at + 8]
            back_ref[m, :, half] = total[at + 16 : at + 24]

    sums = []
    for half in range(2):
        total = ring_total(1, half)
        z_copies[half].wait_recv()
        sums.append(total + zbox[half].astype(F32))
    gg_ref[0] = sums[0][0:64]
    gu_ref[0, 0:32] = sums[0][64:96]
    gu_ref[0, 32:64] = sums[1][0:32]
    gd_ref[0] = sums[1][32:96]

    for at in range(n_x):
        if at:
            over_x(at).wait_send()
        to_pair(at).wait_send()
        to_other(at).wait_send()
    for turn in range(n_x // 2):
        for b in range(2):
            hand_on(turn, b).wait_send()
    for turn in range(n_x // 2):
        mate_own(turn).wait_send()
        mate_other(turn).wait_send()
        for b in range(2):
            cross(turn, b).wait_send()
    for at in range(1, n_x):
        home(at).wait_send()
    xt_copy.wait_send()
    gs_copy.wait_send()

    for part in range(2):
        for half, d in ways:
            for step in range(hops(half, d)):
                ring_copy(part, half, d, step).wait_send()
    for copy in z_copies:
        copy.wait_send()


def write_kernel(count, *refs):
    ins, outs, held = refs[:count], refs[count : 2 * count], refs[2 * count : 3 * count]
    in_sem, out_sem = refs[3 * count :]
    reads = [pltpu.make_async_copy(ins[n], held[n], in_sem.at[n]) for n in range(count)]
    writes = [pltpu.make_async_copy(held[n], outs[n], out_sem.at[n]) for n in range(count)]
    for copy in reads:
        copy.start()
    for n in range(count):
        reads[n].wait()
        writes[n].start()
    for copy in writes:
        copy.wait()


def shards(tokens, cotangent, routes, gate_codes, gate_weight, up_weight, down_weight):
    micro, toks, width = tokens.shape
    n_peer = lax.axis_size("expert")
    n_dp = lax.axis_size("dp")
    hidden = gate_weight.shape[2]
    scale_factor = 1.0 / math.sqrt(n_dp * micro * n_peer * 2)
    n_y = n_dp // 4
    n_x = n_peer // 4
    vmem = pl.BlockSpec(memory_space=pltpu.VMEM)
    hbm = pl.BlockSpec(memory_space=pltpu.HBM)
    anyspace = pl.BlockSpec(memory_space=pl.ANY)
    dma = pltpu.SemaphoreType.DMA
    tok = jax.ShapeDtypeStruct((micro, toks, width), BF16)
    grad = jax.ShapeDtypeStruct((1, width // n_dp, hidden), F32)
    shapes = (tok, tok, grad, grad, grad)
    results = pl.pallas_call(
        functools.partial(kernel, scale_factor, n_dp, n_peer),
        out_shape=shapes,
        in_specs=[hbm] * 7,
        out_specs=(vmem,) * 5,
        scratch_shapes=[
            pltpu.VMEM((micro, 2, toks), jnp.int32),
            pltpu.VMEM((micro, 2, toks), jnp.int32),
            pltpu.VMEM((micro, toks, width), BF16),
            pltpu.VMEM((micro, toks, width), BF16),
            pltpu.VMEM((width, hidden), BF16),
            pltpu.VMEM((width, hidden), BF16),
            pltpu.VMEM((width, hidden), BF16),
            pltpu.VMEM((n_peer // 2, 16, 1024), BF16),
            pltpu.VMEM((n_x, 2, 16, 1024), BF16),
            pltpu.VMEM((n_x, 4, 16, 1024), BF16),
            pltpu.VMEM((4, 128, 1024), BF16),
            pltpu.VMEM((2, 16, 2, 64, 128), BF16),
            pltpu.VMEM((2, 16, 64, 128), BF16),
            pltpu.VMEM((3, 128, hidden), BF16),
            pltpu.VMEM((3, 128, hidden), BF16),
            pltpu.VMEM((n_x, 4, 16, 1024), BF16),
            pltpu.VMEM((n_x // 2, 2, 16, 1024), BF16),
            pltpu.VMEM((n_x // 2, 2, 16, 1024), BF16),
            pltpu.VMEM((n_x // 2, 2, 16, 1024), BF16),
            pltpu.VMEM((n_x, 2, 16, 1024), BF16),
            pltpu.VMEM((n_peer // 2, 16, 1024), BF16),
            pltpu.VMEM((256, 128), BF16),
            pltpu.VMEM((16, 192, hidden), BF16),
            pltpu.VMEM((2, 2, 2, n_y // 2, 96, hidden), BF16),
            pltpu.VMEM((2, 96, hidden), BF16),
            pltpu.VMEM((2, 96, hidden), BF16),
            dma((7,)),
            dma((n_x,)),
            dma((n_x,)),
            dma((n_x,)),
            dma((n_x,)),
            dma((n_x // 2, 2)),
            dma((n_x, 4)),
            dma((n_x // 2, 2)),
            dma((n_x // 2, 2)),
            dma((n_x // 2, 2)),
            dma((n_x,)),
            dma((n_x,)),
            dma((n_x,)),
            dma((2,)),
            dma((2,)),
            dma((2, 2, 2, n_y // 2)),
            dma((2, 2, 2, n_y // 2)),
            dma((2,)),
            dma((2,)),
        ],
        compiler_params=pltpu.CompilerParams(
            collective_id=0, has_side_effects=True, vmem_limit_bytes=56 * 1024 * 1024
        ),
        name="moe_layer",
    )(
        routes.transpose(0, 2, 1),
        gate_codes.transpose(0, 2, 1),
        tokens,
        cotangent,
        gate_weight,
        up_weight,
        down_weight,
    )
    return pl.pallas_call(
        functools.partial(write_kernel, len(shapes)),
        out_shape=shapes,
        in_specs=[anyspace] * len(shapes),
        out_specs=(hbm,) * len(shapes),
        scratch_shapes=[pltpu.VMEM(one.shape, one.dtype) for one in shapes]
        + [dma((len(shapes),)), dma((len(shapes),))],
        name="write_out",
    )(*results)


def solution(mesh):
    tok_spec = P(None, ("dp", "expert"), None)
    w_spec = P("expert", None, None)
    g_spec = P("expert", "dp", None)
    return jax.shard_map(
        shards,
        mesh=mesh,
        in_specs=(tok_spec,) * 4 + (w_spec,) * 3,
        out_specs=(tok_spec,) * 2 + (g_spec,) * 3,
        check_vma=False,
    )
```

```python
import functools
import math

import jax
import jax.numpy as jnp
from jax import lax
from jax.experimental import pallas as pl
from jax.experimental.pallas import tpu as pltpu
from jax.sharding import PartitionSpec as P

MESH = pl.DeviceIdType.MESH
F32 = jnp.float32
BF16 = jnp.bfloat16

ORDER = (0, 1, 7, 2, 6, 3, 5, 4)


def dot(left, right):
    return jnp.dot(left, right, preferred_element_type=F32)


def dot_last(left, right):
    return lax.dot_general(left, right, (((1,), (1,)), ((), ())), preferred_element_type=F32)


def dot_first(left, right):
    return lax.dot_general(left, right, (((0,), (0,)), ((), ())), preferred_element_type=F32)


def iota(shape, axis):
    return lax.broadcasted_iota(jnp.int32, shape, axis)


def route_vectors(route_ref, code_ref):
    row = iota((16, 8), 0)
    lane = iota((16, 8), 1)
    here = [(lane == (row & 7)) & ((row >> 3) == m) for m in range(2)]

    def column(ref, r):
        parts = [jnp.where(here[m], ref[m, r : r + 1, :].astype(F32), 0.0) for m in range(2)]
        return jnp.sum(parts[0] + parts[1], axis=1, keepdims=True)

    spread = iota((16, 128), 0) == (iota((16, 128), 1) & 15)

    def along(col):
        return jnp.sum(jnp.where(spread, col, 0.0), axis=0, keepdims=True)

    cols = [column(route_ref, r) for r in range(2)]
    codes = [column(code_ref, r) for r in range(2)]
    whole = codes[0] + codes[1]
    lanes = jnp.concatenate([along(col) for col in cols], axis=0)
    share = jnp.concatenate([along(code / whole) for code in codes], axis=0)
    return jnp.concatenate(cols, axis=1), lanes, share


def slot_ranks(cols, lanes):
    width = lanes.shape[1]
    tok_col = iota((16, width), 0)
    tok_lane = iota((16, width), 1) & 15
    same = (tok_col >> 3) == (tok_lane >> 3)
    before = same & (tok_col < tok_lane)
    upto = same & (tok_col <= tok_lane)
    col0, col1 = cols[:, 0:1], cols[:, 1:2]
    lane0, lane1 = lanes[0:1, :], lanes[1:2, :]

    def count(mask):
        return jnp.sum(jnp.where(mask, 1.0, 0.0), axis=0, keepdims=True)

    rank0 = count((col0 == lane0) & before) + count((col1 == lane0) & before)
    rank1 = count((col0 == lane1) & upto) + count((col1 == lane1) & before)
    return rank0, rank1


def slot_masks(rows, shift, cols, lanes):
    width = lanes.shape[1]
    rank0, rank1 = slot_ranks(cols, lanes)
    row = iota((rows, width), 0)
    lane = iota((rows, width), 1)
    expert = (row >> shift).astype(F32)
    slot = (row & 1).astype(F32)
    fits = (((row >> 2) & 3) == ((lane >> 4) & 3)) & (((row >> 1) & 1) == ((lane >> 3) & 1))
    mask0 = fits & (lanes[0:1, :] == expert) & (rank0 == slot)
    mask1 = fits & (lanes[1:2, :] == expert) & (rank1 == slot)
    return mask0, mask1


def kernel(
    scale_factor,
    n_dp,
    n_peer,
    route_hbm,
    code_hbm,
    tok_hbm,
    cot_hbm,
    wg_hbm,
    wu_hbm,
    wd_hbm,
    mixed_ref,
    back_ref,
    gg_ref,
    gu_ref,
    gd_ref,
    route_ref,
    code_ref,
    tok_ref,
    cot_ref,
    wg,
    wu,
    wd,
    outbox,
    relay,
    inbox,
    xs,
    yt,
    xt,
    xt_pair,
    gs,
    gs_pair,
    retbox,
    mate_near,
    mate_far,
    crossbox,
    colbox,
    retin,
    comb,
    parts,
    ring,
    zout,
    zbox,
    w_sem,
    xs_sem,
    xr_sem,
    ps_sem,
    os_sem,
    hs_sem,
    pr_sem,
    ms_sem,
    mr_sem,
    qs_sem,
    qr_sem,
    bs_sem,
    br_sem,
    cs_sem,
    cr_sem,
    ys_sem,
    yr_sem,
    zs_sem,
    zr_sem,
):
    k = lax.axis_index("expert")
    i = lax.axis_index("dp")
    n_y = n_dp // 4
    n_x = n_peer // 4
    x, z = k // 4, k % 4
    y, zh, core = i // 4, (i // 2) % 2, i % 2
    pair = y * 4 + zh * 2 + (1 - core)
    zpart = y * 4 + (1 - zh) * 2 + core
    up = ((y + 1) % n_y) * 4 + zh * 2 + core
    down = ((y + n_y - 1) % n_y) * 4 + zh * 2 + core

    loads = (
        (route_hbm, route_ref),
        (code_hbm, code_ref),
        (tok_hbm, tok_ref),
        (cot_hbm, cot_ref),
        (wg_hbm.at[0], wg),
        (wu_hbm.at[0], wu),
        (wd_hbm.at[0], wd),
    )
    loads = [pltpu.make_async_copy(src, dst, w_sem.at[n]) for n, (src, dst) in enumerate(loads)]
    t_copies, w_copies = loads[:4], loads[4:]
    for copy in loads:
        copy.start()

    barrier = pltpu.get_barrier_semaphore()

    for n in range(1, n_x):
        pl.semaphore_signal(
            barrier, inc=1, device_id={"expert": (x + n) % n_x * 4 + z}, device_id_type=MESH
        )
    for n in range(1, 4):
        pl.semaphore_signal(
            barrier, inc=1, device_id={"expert": x * 4 + (z + n) % 4}, device_id_type=MESH
        )
    for other in (pair, zpart, up, down):
        pl.semaphore_signal(barrier, inc=1, device_id={"dp": other}, device_id_type=MESH)

    for copy in t_copies:
        copy.wait()

    cols, all_lanes, all_share = route_vectors(route_ref, code_ref)
    lanes = all_lanes[:, 0:64]
    share = all_share[:, 0:64]
    mask0, mask1 = slot_masks(256, 4, cols, lanes)
    pick = jnp.where(mask0 | mask1, 1.0, 0.0).astype(BF16)
    slot_share = jnp.sum(
        jnp.where(mask0, share[0:1, :], 0.0) + jnp.where(mask1, share[1:2, :], 0.0),
        axis=1,
        keepdims=True,
    )
    is_cot = ((iota((256, 1), 0) >> 2) & 1) == 1
    slot_scale = jnp.where(is_cot, slot_share, 1.0)
    stack = jnp.concatenate(
        [
            ref[m, :, d * 1024 : (d + 1) * 1024]
            for d in range(2)
            for ref in (tok_ref, cot_ref)
            for m in range(2)
        ],
        axis=0,
    )
    outbox[...] = (slot_scale * dot(pick, stack)).astype(BF16).reshape(16, 16, 1024)

    pl.semaphore_wait(barrier, n_x - 1 + 3 + 4)

    def over_x(at):
        return pltpu.make_async_remote_copy(
            src_ref=outbox.at[pl.ds((x + ORDER[at]) % n_x * 2, 2)],
            dst_ref=relay.at[at],
            send_sem=xs_sem.at[at],
            recv_sem=xr_sem.at[at],
            device_id={"expert": (x + ORDER[at]) % n_x * 4 + z},
            device_id_type=MESH,
        )

    def to_pair(at):
        return pltpu.make_async_remote_copy(
            src_ref=relay.at[at, z // 2],
            dst_ref=inbox.at[at, z],
            send_sem=ps_sem.at[at],
            recv_sem=pr_sem.at[at, z],
            device_id={"expert": x * 4 + z + 1 - z % 2 * 2},
            device_id_type=MESH,
        )

    def to_other(at):
        return pltpu.make_async_remote_copy(
            src_ref=relay.at[at, 1 - z // 2],
            dst_ref=inbox.at[at, z],
            send_sem=os_sem.at[at],
            recv_sem=pr_sem.at[at, z],
            device_id={"expert": x * 4 + (1 - z // 2) * 2 + at % 2},
            device_id_type=MESH,
        )

    def hand_on(turn, b):
        at = turn * 2 + z % 2
        source = (1 - z // 2) * 2 + b
        return pltpu.make_async_remote_copy(
            src_ref=inbox.at[at, source],
            dst_ref=inbox.at[at, source],
            send_sem=hs_sem.at[turn, b],
            recv_sem=pr_sem.at[at, source],
            device_id={"expert": x * 4 + z + 1 - z % 2 * 2},
            device_id_type=MESH,
        )

    def arrival(at, source):
        return pltpu.make_async_remote_copy(
            src_ref=inbox.at[at, source],
            dst_ref=inbox.at[at, source],
            send_sem=ps_sem.at[0],
            recv_sem=pr_sem.at[at, source],
            device_id={"expert": x * 4 + z + 1 - z % 2 * 2},
            device_id_type=MESH,
        )

    row = iota((128, 128), 0)
    lane = iota((128, 128), 1)
    order = jnp.where(((row >> 2) & 7) * 16 + (row >> 5) * 4 + (row & 3) == lane, 1.0, 0.0)
    order = order.astype(BF16)

    def forward(at):
        if at:
            over_x(at).wait_recv()
        to_other(at).start()
        to_pair(at).start()
        inbox[at, z] = relay[at, z // 2]

    def relay_turn(turn):
        for b in range(2):
            arrival(turn * 2 + z % 2, (1 - z // 2) * 2 + b).wait_recv()
            hand_on(turn, b).start()

    def sort_rows(g):
        for at in (2 * g, 2 * g + 1):
            arrival(at, z + 1 - z % 2 * 2).wait_recv()
        for b in range(2):
            arrival(2 * g + 1 - z % 2, (1 - z // 2) * 2 + b).wait_recv()
        block = inbox[2 * g : 2 * g + 2].reshape(128, 1024)
        sorted_rows = dot(order, block).astype(BF16)
        for q in range(4):
            xs[q, g * 32 : (g + 1) * 32] = sorted_rows[q * 32 : (q + 1) * 32]

    relay[0] = outbox[pl.ds(x * 2, 2)]
    over_x(1).start()
    over_x(2).start()
    forward(0)
    for at in range(3, n_x):
        over_x(at).start()
    forward(1)
    forward(2)

    along = iota((2, 128), 1)
    weight = jnp.where(((along >> 4) & 1) == 0, all_share, 1.0)
    high = weight.astype(BF16).astype(F32)
    weight = jnp.where(along < 64, high, weight - high)
    mask0, mask1 = slot_masks(256, 4, cols, all_lanes)
    comb[...] = (
        jnp.where(mask0, weight[0:1, :], 0.0) + jnp.where(mask1, weight[1:2, :], 0.0)
    ).astype(BF16)

    relay_turn(0)
    forward(3)
    forward(4)
    relay_turn(1)
    forward(5)
    forward(6)
    sort_rows(0)
    forward(7)
    relay_turn(2)
    sort_rows(1)
    relay_turn(3)
    sort_rows(2)
    sort_rows(3)

    for q in range(4):
        turned = jnp.transpose(xs[q])
        xt[q % 2, (q // 2) * 8 : (q // 2 + 1) * 8] = turned.reshape(8, 2, 64, 128)
    xt_copy = pltpu.make_async_remote_copy(
        src_ref=xt.at[:, :, 1 - core],
        dst_ref=xt_pair,
        send_sem=cs_sem.at[0],
        recv_sem=cr_sem.at[0],
        device_id={"dp": pair},
        device_id_type=MESH,
    )
    xt_copy.start()

    for copy in w_copies:
        copy.wait()

    pre_gate = dot(xs[0], wg[0:1024]) + dot(xs[2], wg[1024:2048])
    pre_up = dot(xs[0], wu[0:1024]) + dot(xs[2], wu[1024:2048])
    grad_hidden = dot(xs[1], wd[0:1024]) + dot(xs[3], wd[1024:2048])
    sigma = jax.nn.sigmoid(pre_gate)
    activ = pre_gate * sigma
    hidden = (activ * pre_up).astype(BF16)
    grad_gate = (grad_hidden * pre_up * sigma * (1.0 + pre_gate * (1.0 - sigma))).astype(BF16)
    grad_up = (grad_hidden * activ).astype(BF16)
    gs[0] = grad_gate
    gs[1] = grad_up
    gs[2] = hidden
    gs_copy = pltpu.make_async_remote_copy(
        src_ref=gs,
        dst_ref=gs_pair,
        send_sem=cs_sem.at[1],
        recv_sem=cr_sem.at[1],
        device_id={"dp": pair},
        device_id_type=MESH,
    )
    gs_copy.start()

    def outputs(d):
        half = slice(d * 1024, (d + 1) * 1024)
        yt[:, d * 256 : d * 256 + 128] = dot(wd[half], turned_hidden).astype(BF16)
        yt[:, d * 256 + 128 : d * 256 + 256] = (
            dot(wg[half], turned_gate) + dot(wu[half], turned_up)
        ).astype(BF16)

    xt_copy.wait_recv()
    gs_copy.wait_recv()

    def make_parts(*steps):
        pairs = [pl.ds((y + step) % n_y * 2, 2) for step in steps]
        for n in range(3):
            a = 0 if n < 2 else 1
            left = [
                jnp.concatenate(
                    [xt[a, two, core].reshape(128, 128), xt_pair[a, two].reshape(128, 128)], axis=1
                )
                for two in pairs
            ]
            right = jnp.concatenate([gs[n], gs_pair[n]], axis=0)
            part = (dot(jnp.concatenate(left, axis=0), right) * scale_factor).astype(BF16)
            for m, two in enumerate(pairs):
                rows = part[m * 128 : (m + 1) * 128].reshape(2, 64, part.shape[1])
                parts[two, n * 64 : (n + 1) * 64] = rows

    ways = [(half, d) for half in range(2) for d in range(2)]

    def hops(half, d):
        return n_y // 2 if half == d else (n_y - 1) // 2

    def own_piece(part, half, step):
        at = (y + step) % n_y * 2 + (1 - zh if part == 0 else zh)
        return parts.at[at, pl.ds(half * 96, 96)]

    def ring_copy(part, half, d, step, source=None):
        slot = ring.at[part, half, d, step]
        return pltpu.make_async_remote_copy(
            src_ref=slot if source is None else source,
            dst_ref=slot,
            send_sem=ys_sem.at[part, half, d, step],
            recv_sem=yr_sem.at[part, half, d, step],
            device_id={"dp": up if d == 0 else down},
            device_id_type=MESH,
        )

    def ring_send(part, step):
        for half, d in ways:
            left = hops(half, d) - step
            if left > 0:
                source = own_piece(part, half, left if d == 0 else n_y - left)
                if step:
                    ring_copy(part, half, d, step - 1).wait_recv()
                    total = ring[part, half, d, step - 1].astype(F32) + source[...].astype(F32)
                    ring[part, half, d, step - 1] = total.astype(BF16)
                    source = ring.at[part, half, d, step - 1]
                ring_copy(part, half, d, step, source).start()

    def ring_total(part, half):
        total = own_piece(part, half, 0)[...].astype(F32)
        for d in range(2):
            ring_copy(part, half, d, hops(half, d) - 1).wait_recv()
            total = total + ring[part, half, d, hops(half, d) - 1].astype(F32)
        return total

    make_parts(4, 3, n_y - 3)
    ring_send(0, 0)

    turned_hidden = jnp.transpose(hidden)
    turned_gate = jnp.transpose(grad_gate)
    turned_up = jnp.transpose(grad_up)
    outputs(0)
    outputs(1)
    row = iota((512, 512), 0)
    lane = iota((512, 512), 1)
    back_order = jnp.where(((row >> 2) & 3) * 128 + (row >> 4) * 4 + (row & 3) == lane, 1.0, 0.0)
    back_order = back_order.astype(BF16)
    for h in range(2):
        half = slice(h * 512, (h + 1) * 512)
        block = dot_last(back_order, yt[half]).astype(BF16)
        retbox[:, :, :, half] = block.reshape(n_x, 4, 16, 512)

    side, odd = z // 2, z % 2
    far = (1 - side) * 2
    mate = {"expert": x * 4 + z + 1 - odd * 2}

    def mate_own(turn):
        return pltpu.make_async_remote_copy(
            src_ref=retbox.at[pl.ds(2 * turn, 2), z + 1 - odd * 2],
            dst_ref=mate_near.at[turn],
            send_sem=ms_sem.at[turn, 0],
            recv_sem=mr_sem.at[turn, 0],
            device_id=mate,
            device_id_type=MESH,
        )

    def mate_other(turn):
        return pltpu.make_async_remote_copy(
            src_ref=retbox.at[2 * turn + 1 - odd, pl.ds(far, 2)],
            dst_ref=mate_far.at[turn],
            send_sem=ms_sem.at[turn, 1],
            recv_sem=mr_sem.at[turn, 1],
            device_id=mate,
            device_id_type=MESH,
        )

    def cross(turn, b):
        return pltpu.make_async_remote_copy(
            src_ref=crossbox.at[turn, b],
            dst_ref=colbox.at[2 * turn + odd, side],
            send_sem=qs_sem.at[turn, b],
            recv_sem=qr_sem.at[2 * turn + odd],
            device_id={"expert": x * 4 + far + b},
            device_id_type=MESH,
        )

    def cross_arrival(at):
        return pltpu.make_async_remote_copy(
            src_ref=colbox.at[at, 1 - side],
            dst_ref=colbox.at[at, 1 - side],
            send_sem=qs_sem.at[0, 0],
            recv_sem=qr_sem.at[at],
            device_id=mate,
            device_id_type=MESH,
        )

    def home(at):
        return pltpu.make_async_remote_copy(
            src_ref=colbox.at[at],
            dst_ref=retin.at[pl.ds(x * 2, 2)],
            send_sem=bs_sem.at[at],
            recv_sem=br_sem.at[at],
            device_id={"expert": (x + n_x - ORDER[at]) % n_x * 4 + z},
            device_id_type=MESH,
        )

    def home_arrival(at):
        return pltpu.make_async_remote_copy(
            src_ref=colbox.at[at],
            dst_ref=retin.at[pl.ds((x + ORDER[at]) % n_x * 2, 2)],
            send_sem=bs_sem.at[at],
            recv_sem=br_sem.at[at],
            device_id=mate,
            device_id_type=MESH,
        )

    def sum_turn(turn):
        mate_own(turn).wait_recv()
        mate_other(turn).wait_recv()
        two = pl.ds(2 * turn, 2)
        colbox[two, side] = (retbox[two, z].astype(F32) + mate_near[turn].astype(F32)).astype(BF16)
        crossbox[turn] = (
            retbox[2 * turn + odd, pl.ds(far, 2)].astype(F32) + mate_far[turn].astype(F32)
        ).astype(BF16)
        for b in range(2):
            cross(turn, b).start()

    def home_turn(turn):
        for at in (2 * turn + 1, 2 * turn):
            cross_arrival(at).wait_recv()
            if at:
                home(at).start()
            else:
                retin[pl.ds(x * 2, 2)] = colbox[0]

    for turn in (3, 2, 1, 0):
        mate_other(turn).start()
        mate_own(turn).start()
    make_parts(2, n_y - 2)

    z_copies = [
        pltpu.make_async_remote_copy(
            src_ref=zout.at[half],
            dst_ref=zbox.at[half],
            send_sem=zs_sem.at[half],
            recv_sem=zr_sem.at[half],
            device_id={"dp": zpart},
            device_id_type=MESH,
        )
        for half in range(2)
    ]
    ring_send(0, 1)
    ring_send(1, 0)
    make_parts(1, n_y - 1, 0)
    sum_turn(3)
    ring_send(0, 2)
    ring_send(1, 1)
    sum_turn(2)
    home_turn(3)
    sum_turn(1)
    home_turn(2)
    ring_send(0, 3)
    ring_send(1, 2)
    sum_turn(0)
    home_turn(1)
    for half in range(2):
        zout[half] = ring_total(0, half).astype(BF16)
        z_copies[half].start()
    ring_send(1, 3)

    home_turn(0)
    for at in range(n_x - 1, 0, -1):
        home_arrival(at).wait_recv()
    both = dot_first(comb[...], retin[...].reshape(256, 1024))
    total = (both[0:64] + both[64:128]).astype(BF16)
    for m in range(2):
        for d in range(2):
            half = slice(d * 1024, (d + 1) * 1024)
            at = d * 32 + m * 8
            mixed_ref[m, :, half] = total[at : at + 8]
            back_ref[m, :, half] = total[at + 16 : at + 24]

    sums = []
    for half in range(2):
        total = ring_total(1, half)
        z_copies[half].wait_recv()
        sums.append(total + zbox[half].astype(F32))
    gg_ref[0] = sums[0][0:64]
    gu_ref[0, 0:32] = sums[0][64:96]
    gu_ref[0, 32:64] = sums[1][0:32]
    gd_ref[0] = sums[1][32:96]

    for at in range(n_x):
        if at:
            over_x(at).wait_send()
        to_pair(at).wait_send()
        to_other(at).wait_send()
    for turn in range(n_x // 2):
        for b in range(2):
            hand_on(turn, b).wait_send()
    for turn in range(n_x // 2):
        mate_own(turn).wait_send()
        mate_other(turn).wait_send()
        for b in range(2):
            cross(turn, b).wait_send()
    for at in range(1, n_x):
        home(at).wait_send()
    xt_copy.wait_send()
    gs_copy.wait_send()

    for part in range(2):
        for half, d in ways:
            for step in range(hops(half, d)):
                ring_copy(part, half, d, step).wait_send()
    for copy in z_copies:
        copy.wait_send()


def write_kernel(count, *refs):
    ins, outs, held = refs[:count], refs[count : 2 * count], refs[2 * count : 3 * count]
    in_sem, out_sem = refs[3 * count :]
    reads = [pltpu.make_async_copy(ins[n], held[n], in_sem.at[n]) for n in range(count)]
    writes = [pltpu.make_async_copy(held[n], outs[n], out_sem.at[n]) for n in range(count)]
    for copy in reads:
        copy.start()
    for n in range(count):
        reads[n].wait()
        writes[n].start()
    for copy in writes:
        copy.wait()


def shards(tokens, cotangent, routes, gate_codes, gate_weight, up_weight, down_weight):
    micro, toks, width = tokens.shape
    n_peer = lax.axis_size("expert")
    n_dp = lax.axis_size("dp")
    hidden = gate_weight.shape[2]
    scale_factor = 1.0 / math.sqrt(n_dp * micro * n_peer * 2)
    n_y = n_dp // 4
    n_x = n_peer // 4
    vmem = pl.BlockSpec(memory_space=pltpu.VMEM)
    hbm = pl.BlockSpec(memory_space=pltpu.HBM)
    anyspace = pl.BlockSpec(memory_space=pl.ANY)
    dma = pltpu.SemaphoreType.DMA
    tok = jax.ShapeDtypeStruct((micro, toks, width), BF16)
    grad = jax.ShapeDtypeStruct((1, width // n_dp, hidden), F32)
    shapes = (tok, tok, grad, grad, grad)
    results = pl.pallas_call(
        functools.partial(kernel, scale_factor, n_dp, n_peer),
        out_shape=shapes,
        in_specs=[hbm] * 7,
        out_specs=(vmem,) * 5,
        scratch_shapes=[
            pltpu.VMEM((micro, 2, toks), jnp.int32),
            pltpu.VMEM((micro, 2, toks), jnp.int32),
            pltpu.VMEM((micro, toks, width), BF16),
            pltpu.VMEM((micro, toks, width), BF16),
            pltpu.VMEM((width, hidden), BF16),
            pltpu.VMEM((width, hidden), BF16),
            pltpu.VMEM((width, hidden), BF16),
            pltpu.VMEM((n_peer // 2, 16, 1024), BF16),
            pltpu.VMEM((n_x, 2, 16, 1024), BF16),
            pltpu.VMEM((n_x, 4, 16, 1024), BF16),
            pltpu.VMEM((4, 128, 1024), BF16),
            pltpu.VMEM((1024, 512), BF16),
            pltpu.VMEM((2, 16, 2, 64, 128), BF16),
            pltpu.VMEM((2, 16, 64, 128), BF16),
            pltpu.VMEM((3, 128, hidden), BF16),
            pltpu.VMEM((3, 128, hidden), BF16),
            pltpu.VMEM((n_x, 4, 16, 1024), BF16),
            pltpu.VMEM((n_x // 2, 2, 16, 1024), BF16),
            pltpu.VMEM((n_x // 2, 2, 16, 1024), BF16),
            pltpu.VMEM((n_x // 2, 2, 16, 1024), BF16),
            pltpu.VMEM((n_x, 2, 16, 1024), BF16),
            pltpu.VMEM((n_peer // 2, 16, 1024), BF16),
            pltpu.VMEM((256, 128), BF16),
            pltpu.VMEM((16, 192, hidden), BF16),
            pltpu.VMEM((2, 2, 2, n_y // 2, 96, hidden), BF16),
            pltpu.VMEM((2, 96, hidden), BF16),
            pltpu.VMEM((2, 96, hidden), BF16),
            dma((7,)),
            dma((n_x,)),
            dma((n_x,)),
            dma((n_x,)),
            dma((n_x,)),
            dma((n_x // 2, 2)),
            dma((n_x, 4)),
            dma((n_x // 2, 2)),
            dma((n_x // 2, 2)),
            dma((n_x // 2, 2)),
            dma((n_x,)),
            dma((n_x,)),
            dma((n_x,)),
            dma((2,)),
            dma((2,)),
            dma((2, 2, 2, n_y // 2)),
            dma((2, 2, 2, n_y // 2)),
            dma((2,)),
            dma((2,)),
        ],
        compiler_params=pltpu.CompilerParams(
            collective_id=0, has_side_effects=True, vmem_limit_bytes=56 * 1024 * 1024
        ),
        name="moe_layer",
    )(
        routes.transpose(0, 2, 1),
        gate_codes.transpose(0, 2, 1),
        tokens,
        cotangent,
        gate_weight,
        up_weight,
        down_weight,
    )
    return pl.pallas_call(
        functools.partial(write_kernel, len(shapes)),
        out_shape=shapes,
        in_specs=[anyspace] * len(shapes),
        out_specs=(hbm,) * len(shapes),
        scratch_shapes=[pltpu.VMEM(one.shape, one.dtype) for one in shapes]
        + [dma((len(shapes),)), dma((len(shapes),))],
        name="write_out",
    )(*results)


def solution(mesh):
    tok_spec = P(None, ("dp", "expert"), None)
    w_spec = P("expert", None, None)
    g_spec = P("expert", "dp", None)
    return jax.shard_map(
        shards,
        mesh=mesh,
        in_specs=(tok_spec,) * 4 + (w_spec,) * 3,
        out_specs=(tok_spec,) * 2 + (g_spec,) * 3,
        check_vma=False,
    )
```
